768 devices in a mesh: dp: 32 (over y, x), expert: 12 (over z), tensor: 2 (over core).
Axes of the slice: x: 4, y: 8, z: 12, core: 2. Of those that a mesh axis runs over, the one named last changes fastest.
Arguments:
- tokens: bfloat16 [98304, 2048], P(('dp', 'expert'), 'tensor'), may hold values from -6 to 6
- cotangent: bfloat16 [98304, 2048], P(('dp', 'expert'), 'tensor'), may hold values from -6 to 6
- route_ids: int32 [98304, 8], P(('dp', 'expert')), may hold values from 0 to 127, all different within a row; in each aligned block of 256 rows (0 to 255, 256 to 511, ...) at most 24 rows name the same one
- gate_codes: int32 [98304, 8], P(('dp', 'expert')), may hold values from 1 to 65535
- w_gate: bfloat16 [12, 2048, 768], P('expert', None, 'tensor'), may hold values from -0.125 to 0.125
- w_up: bfloat16 [12, 2048, 768], P('expert', None, 'tensor'), may hold values from -0.125 to 0.125
- w_down: bfloat16 [12, 2048, 768], P('expert', None, 'tensor'), may hold values from -0.21875 to 0.21875
Outputs:
- token_grad: bfloat16 [98304, 2048], P(('dp', 'expert'), 'tensor')
- grad_gate: float32 [12, 2048, 768], P('expert', 'dp', 'tensor')
- grad_up: float32 [12, 2048, 768], P('expert', 'dp', 'tensor')
- grad_down: float32 [12, 2048, 768], P('expert', 'dp', 'tensor')
The draws below stay inside these ranges and needn't reach their ends.
Inputs may be any that keep to these rules, and one draw needn't show every extreme that they name: `route_ids`: each row names 8 different experts. Within the rows of one device (aligned blocks of 256 rows) no expert is named by more than 24 rows, and in every draw some expert is named by exactly 24 rows of some block.
All inputs are finite; a program needn't handle non-finite values.
Results may differ from the reference program's by a relative error of at most 0.02.
Values may be sent and summed in bfloat16 or wider, within the bound.
A program may use at most 64 MiB of HBM per device.

```python
import math
import jax
import jax.numpy as jnp
import numpy as np
from jax import lax

D = 2048
FF = 768
ROUTED = 128
TOP = 8
TOK_DEV = 256
EXPERTS = 12
CAP = 24
TOKENS = 98304
N_DP = 32
N_EXPERT = 12


def place_ends(drawn, stream_key, low, largest):
    dims = drawn.shape
    place = [jax.random.randint(jax.random.fold_in(stream_key, axis), (), 0, dims[axis]) for axis in range(len(dims))]
    drawn = drawn.at[tuple(place)].set(low)
    longest = dims.index(max(dims))
    place[longest] = (place[longest] + 1) % dims[longest]
    return drawn.at[tuple(place)].set(largest)


def steps_of(key, shape, cuts, low, high):
    def one(dim, blocks):
        steps = jax.random.uniform(jax.random.fold_in(jax.random.fold_in(key, 6), dim), (blocks,), jnp.float32, low / len(cuts), high / len(cuts))
        return jnp.repeat(jnp.exp(steps), shape[dim] // blocks).reshape((-1,) + (1,) * (len(shape) - dim - 1))

    loudness = one(*cuts[0])
    for cut in cuts[1:]:
        loudness = loudness * one(*cut)
    return loudness


def assign_block(key, own, number, rows, count, top, reach, skew):
    sequence = jax.random.permutation(key, count)
    crowded, ordinary = portions_of(count, rows * top, reach, skew, True), portions_of(count, rows * top, reach, skew, False)
    places = jnp.arange(count)

    def named(sizes, turn):
        used = int((sizes > 0).sum())
        fixed = max(1, used // 4)
        moved = fixed + (places - fixed + turn * (used - fixed)) % max(1, count - fixed)
        return jnp.zeros((count,), jnp.int32).at[sequence[jnp.where(places < fixed, places, moved)]].set(jnp.asarray(sizes, jnp.int32))

    sizes = jnp.where(number % 4 == 0, named(crowded, number // 4), named(ordinary, number - number // 4 - 1))
    mixed = jax.random.permutation(jax.random.fold_in(own, 3), count)
    donor, sink = mixed[0:count // 2 * 2:2], mixed[1:count // 2 * 2:2]
    margin = jnp.minimum(sizes[donor] - 1, reach - sizes[sink]) // 2
    margin = jnp.where((donor == sequence[0]) | (sink == sequence[0]) | (sizes[sink] == 0), 0, jnp.maximum(margin, 0))
    moved = jax.random.randint(jax.random.fold_in(own, 4), (count // 2,), 0, 1 << 20) % (margin + 1)
    sizes = sizes.at[donor].add(-moved).at[sink].add(moved)
    members = jnp.searchsorted(jnp.cumsum(sizes), jnp.arange(rows * top), side="right").astype(jnp.int32)
    grid = members.reshape(top, rows).T
    grid = grid[jax.random.permutation(jax.random.fold_in(own, 1), rows)]
    turn = jax.random.randint(jax.random.fold_in(own, 2), (rows, 1), 0, top)
    return jnp.take_along_axis(grid, (jnp.arange(top)[None, :] + turn) % top, axis=1)


def portions_of(count, total, bound, skew, full):
    loads = [(1 << 20) // math.isqrt(rank ** skew) + 1 for rank in range(1, count + 1)]
    largest = bound if full else min(bound, max(-(-total // count), total * loads[0] // sum(loads)))
    least = 1 if total - largest >= count - 1 else 0
    given, surplus = [largest] + [least] * (count - 1), total - largest - least * (count - 1)
    while surplus > 0:
        movable = [i for i in range(1, count) if given[i] < largest] or [i for i in range(1, count) if given[i] < bound]
        mass, remaining = sum([loads[i] for i in movable]), surplus
        for i in movable:
            addition = min(bound - given[i], max(1, remaining * loads[i] // mass), surplus)
            given[i] = given[i] + addition
            surplus = surplus - addition
    return np.array(given)


def gaussian(stream_key, extent, scale, reach, shards=(), kind=jnp.bfloat16):
    entries = scale * jax.random.normal(stream_key, extent, jnp.float32)
    if shards:
        entries = entries * steps_of(stream_key, extent, shards, -0.22, 0.18)
    return jnp.clip(entries, -reach, reach).astype(kind)


def setup_inputs(seed: int = 0) -> dict:
    key_list = jax.random.split(jax.random.key(seed), 8)
    tokens = gaussian(key_list[0], (TOKENS, D), 1.0, 6.0, ((0, 384), (1, 2)))
    cotangent = gaussian(key_list[1], (TOKENS, D), 1.0, 6.0, ((0, 384), (1, 2)))
    route_ids_keys = jax.random.split(jax.random.fold_in(key_list[2], 1), TOKENS // TOK_DEV)
    route_ids_turns = jax.random.permutation(jax.random.fold_in(key_list[2], 3), TOKENS // TOK_DEV)
    route_ids = jax.vmap(lambda own, number: assign_block(jax.random.fold_in(key_list[2], 2), own, number, TOK_DEV, ROUTED, TOP, CAP, 2))(route_ids_keys, route_ids_turns).reshape((TOKENS, TOP))
    gate_codes = place_ends(jax.random.randint(key_list[3], (TOKENS, TOP), 1, 65536), jax.random.fold_in(key_list[3], 1), 1, 65535).astype(jnp.int32)
    w_gate = gaussian(key_list[4], (EXPERTS, D, FF), D ** -0.5, 0.125, ((0, 12), (2, 2)))
    w_up = gaussian(key_list[5], (EXPERTS, D, FF), D ** -0.5, 0.125, ((0, 12), (2, 2)))
    w_down = gaussian(key_list[6], (EXPERTS, D, FF), FF ** -0.5, 0.21875, ((0, 12), (2, 2)))
    return {"tokens": tokens, "cotangent": cotangent, "route_ids": route_ids, "gate_codes": gate_codes, "w_gate": w_gate, "w_up": w_up, "w_down": w_down}


def reference(tokens, cotangent, route_ids, gate_codes, w_gate, w_up, w_down):
    groups = N_DP * N_EXPERT
    routes_block = TOK_DEV * TOP
    flat_ids = route_ids.reshape(groups, routes_block)
    onehot = (flat_ids[:, :, None] == jnp.arange(EXPERTS, dtype=jnp.int32)[None, None, :]).astype(jnp.int32)
    earlier = jnp.cumsum(onehot, axis=1) - onehot
    position = jnp.sum(earlier * onehot, axis=2).astype(jnp.int32)
    group_index = jnp.arange(groups, dtype=jnp.int32)[:, None]
    dp_index = group_index // N_EXPERT
    source = group_index % N_EXPERT
    slot_total = EXPERTS * N_DP * N_EXPERT * CAP
    slot = ((flat_ids * N_DP + dp_index) * N_EXPERT + source) * CAP + position
    slot = jnp.where(flat_ids < EXPERTS, slot, slot_total).astype(jnp.int32)
    token_index = group_index * TOK_DEV + jnp.arange(routes_block, dtype=jnp.int32)[None, :] // TOP
    slot_flat = slot.reshape(-1)
    slot_token = jnp.zeros((slot_total,), jnp.int32).at[slot_flat].set(token_index.reshape(-1).astype(jnp.int32), mode="drop")
    gate_values = gate_codes.astype(jnp.float32).reshape(-1) / 65536.0
    slot_gate = jnp.zeros((slot_total,), jnp.float32).at[slot_flat].set(gate_values, mode="drop")
    slot_filled = jnp.zeros((slot_total,), jnp.float32).at[slot_flat].set(1.0, mode="drop")
    slot_rows = N_EXPERT * CAP
    token_table = slot_token.reshape(EXPERTS, N_DP, slot_rows)
    gate_table = slot_gate.reshape(EXPERTS, N_DP, slot_rows)
    filled_table = slot_filled.reshape(EXPERTS, N_DP, slot_rows)

    def one_expert(pieces):
        rows_token, rows_gate, rows_filled, wg, wu, wd = pieces
        moved = jnp.where(rows_filled[:, :, None] > 0, tokens[rows_token], jnp.zeros((), jnp.bfloat16)).astype(jnp.bfloat16)
        scaled = (rows_gate[:, :, None] * cotangent[rows_token].astype(jnp.float32)).astype(jnp.bfloat16)
        moved32 = moved.astype(jnp.float32)
        scaled32 = scaled.astype(jnp.float32)
        wg32 = wg.astype(jnp.float32)
        wu32 = wu.astype(jnp.float32)
        wd32 = wd.astype(jnp.float32)
        pre_gate = jnp.einsum('prd,df->prf', moved32, wg32)
        pre_up = jnp.einsum('prd,df->prf', moved32, wu32)
        sigma_gate = jax.nn.sigmoid(pre_gate)
        activated = pre_gate * sigma_gate
        hidden = (activated * pre_up).astype(jnp.bfloat16)
        d_hidden = jnp.einsum('prd,df->prf', scaled32, wd32)
        d_gate = (d_hidden * pre_up * sigma_gate * (1.0 + pre_gate * (1.0 - sigma_gate))).astype(jnp.bfloat16)
        d_up = (d_hidden * activated).astype(jnp.bfloat16)
        d_gate32 = d_gate.astype(jnp.float32)
        d_up32 = d_up.astype(jnp.float32)
        route_grad = (jnp.einsum('prf,df->prd', d_gate32, wg32) + jnp.einsum('prf,df->prd', d_up32, wu32)).astype(jnp.bfloat16)
        part_gate = jnp.einsum('prd,prf->pdf', moved32, d_gate32).astype(jnp.bfloat16)
        part_up = jnp.einsum('prd,prf->pdf', moved32, d_up32).astype(jnp.bfloat16)
        part_down = jnp.einsum('prd,prf->pdf', scaled32, hidden.astype(jnp.float32)).astype(jnp.bfloat16)
        part_gate, part_up, part_down = lax.optimization_barrier((part_gate, part_up, part_down))
        return (route_grad,
                jnp.sum(part_gate.astype(jnp.float32), axis=0),
                jnp.sum(part_up.astype(jnp.float32), axis=0),
                jnp.sum(part_down.astype(jnp.float32), axis=0))

    route_grads, grad_gate, grad_up, grad_down = lax.map(one_expert, (token_table, gate_table, filled_table, w_gate, w_up, w_down))
    contributions = route_grads.reshape(slot_total, D).astype(jnp.float32) * slot_filled[:, None]
    token_grad = jnp.zeros((TOKENS, D), jnp.float32).at[slot_token].add(contributions).astype(jnp.bfloat16)
    return token_grad, grad_gate, grad_up, grad_down
```

```python
import functools

import jax
import jax.numpy as jnp
from jax import lax
from jax.experimental import pallas as pl
from jax.experimental.pallas import tpu as pltpu
from jax.sharding import PartitionSpec as P

MESH = pl.DeviceIdType.MESH
F32 = jnp.float32
BF16 = jnp.bfloat16
NX, NY, NZ = 4, 8, 12
CAP = 24
SLOTS = NZ * CAP
GATE_UNIT = 65536.0


def chains_of(n):
    half = n // 2
    listed, slot = [], 0
    for sign, part, length in ((1, 0, half), (-1, 1, half), (1, 1, half - 1), (-1, 0, half - 1)):
        listed.append((sign, part, length, slot))
        slot += length
    return listed


def kernel(
    ids_ref, codes_ref, tok_hbm, cot_hbm, wg_hbm, wu_hbm, wd_hbm,
    out_tok, out_gate, out_up, out_down,
    tok, cot, wg, wu, wd, place, send_x, send_c, recv_x, recv_c, x_full, c_full, pre_gate, pre_up,
    d_both, hidden, own_part, peer_out, peer_in, back_out, back_in,
    pa, pb, pa2, pb2, ra, rb, ra2, rb2,
    in_sem, zx_s, zx_r, zc_s, zc_r, tx_s, tx_r, tc_s, tc_r, loc_sem, p_s, p_r, back_s, back_r,
    ra_s, ra_r, rb_s, rb_r, ra2_s, ra2_r, rb2_s, rb2_r,
):
    dp = lax.axis_index("dp")
    z = lax.axis_index("expert")
    c = lax.axis_index("tensor")
    y, x = dp // NX, dp % NX
    peer = 1 - c
    cols = tok.shape[1]

    loads = [
        pltpu.make_async_copy(src, dst, in_sem.at[i])
        for i, (src, dst) in enumerate(((tok_hbm, tok), (cot_hbm, cot), (wg_hbm, wg), (wu_hbm, wu), (wd_hbm, wd)))
    ]
    for load in loads:
        load.start()

    def at_z(k):
        return (dp, k, c)

    def at_x(k):
        return (y * NX + k, z, c)

    def at_y(k):
        return (k * NX + x, z, c)

    at_peer = (dp, z, peer)

    barrier = pltpu.get_barrier_semaphore()

    def greet(i, carry):
        pl.semaphore_signal(barrier, inc=1, device_id=at_z(lax.rem(z + i, NZ)), device_id_type=MESH)
        return carry

    lax.fori_loop(1, NZ, greet, 0)
    pl.semaphore_signal(barrier, inc=1, device_id=at_peer, device_id_type=MESH)
    for step in (1, NX - 1):
        pl.semaphore_signal(barrier, inc=1, device_id=at_x(lax.rem(x + step, NX)), device_id_type=MESH)
    for step in (1, NY - 1):
        pl.semaphore_signal(barrier, inc=1, device_id=at_y(lax.rem(y + step, NY)), device_id_type=MESH)

    count = ids_ref.shape[1]
    expert_row = lax.broadcasted_iota(jnp.int32, (16, count), 0)
    match = jnp.zeros((16, count), F32)
    gates = jnp.zeros((16, count), F32)
    for k in range(ids_ref.shape[0]):
        same = ids_ref[k : k + 1, :] == expert_row
        match = match + jnp.where(same, 1.0, 0.0)
        gates = gates + jnp.where(same, codes_ref[k : k + 1, :].astype(F32) / GATE_UNIT, 0.0)
    before = jnp.where(
        lax.broadcasted_iota(jnp.int32, (count, count), 0) < lax.broadcasted_iota(jnp.int32, (count, count), 1),
        1.0, 0.0,
    ).astype(BF16)
    position = jnp.dot(match.astype(BF16), before, preferred_element_type=F32)
    position = jnp.where(match > 0.5, position, -1.0)
    slot_row = lax.broadcasted_iota(jnp.int32, (CAP, count), 0).astype(F32)
    pieces, slot_gates = [], []
    for e in range(NZ):
        piece = jnp.where(position[e : e + 1, :] == slot_row, 1.0, 0.0)
        pieces.append(piece)
        slot_gates.append(jnp.sum(piece * gates[e : e + 1, :], axis=1, keepdims=True))
    place[...] = jnp.concatenate(pieces, axis=0).astype(BF16)
    slot_gate = jnp.concatenate(slot_gates, axis=0)

    def z_copy(src, dst, send, recv, target, slab):
        return pltpu.make_async_remote_copy(
            src_ref=src.at[target], dst_ref=dst.at[c, slab], send_sem=send.at[target], recv_sem=recv.at[slab],
            device_id=at_z(target), device_id_type=MESH,
        )

    def t_copy(src, dst, half, send, recv, slab):
        return pltpu.make_async_remote_copy(
            src_ref=src, dst_ref=dst.at[half, slab], send_sem=send.at[slab], recv_sem=recv.at[slab],
            device_id=at_peer, device_id_type=MESH,
        )

    def turn(i):
        step = (i + 1) // 2
        return lax.rem(z + NZ + jnp.where(i % 2 == 1, step, -step), NZ)

    def gather(table, buffer, scale):
        for block in range(cols // 256):
            part = jnp.dot(place[...], table[:, block * 256 : block * 256 + 256], preferred_element_type=F32)
            if scale is not None:
                part = scale * part
            for e in range(NZ):
                buffer[e, :, block * 256 : block * 256 + 256] = part[e * CAP : (e + 1) * CAP, :].astype(BF16)

    def send_all(src, dst, zs, zr, ts, tr, own):
        def one(i, carry):
            z_copy(src, dst, zs, zr, turn(i), z).start()
            return carry

        lax.fori_loop(1, NZ, one, 0)
        t_copy(src.at[z], dst, c, ts, tr, z).start()
        own_copy = pltpu.make_async_copy(src.at[z], dst.at[c, z], loc_sem.at[own])
        own_copy.start()
        return own_copy

    loads[0].wait()
    gather(tok, send_x, None)
    pl.semaphore_wait(barrier, NZ - 1 + 5)
    own_x = send_all(send_x, recv_x, zx_s, zx_r, tx_s, tx_r, 0)
    loads[1].wait()
    gather(cot, send_c, slot_gate)
    own_c = send_all(send_c, recv_c, zc_s, zc_r, tc_s, tc_r, 1)

    def pass_on(src, dst, zs, zr, ts, tr):
        def one(i, carry):
            slab = turn(i)
            z_copy(src, dst, zs, zr, slab, slab).wait_recv()
            t_copy(dst.at[c, slab], dst, c, ts, tr, slab).start()
            return carry

        lax.fori_loop(1, NZ, one, 0)

    def from_peer(src, dst, ts, tr):
        def one(i, carry):
            t_copy(src.at[i], dst, peer, ts, tr, i).wait_recv()
            return carry

        lax.fori_loop(0, NZ, one, 0)

    def assemble(slabs, full):
        for half in range(2):
            def one(b, carry, half=half):
                col = pl.multiple_of(b * 256, 256)
                rows = [slabs[half, e, :, pl.ds(col, 256)].astype(F32) for e in range(NZ)]
                full[:, pl.ds(pl.multiple_of(half * cols + b * 256, 256), 256)] = jnp.concatenate(rows, axis=0).astype(BF16)
                return carry

            lax.fori_loop(0, cols // 256, one, 0)

    pass_on(send_x, recv_x, zx_s, zx_r, tx_s, tx_r)
    own_x.wait()
    from_peer(send_x, recv_x, tx_s, tx_r)
    assemble(recv_x, x_full)
    loads[2].wait()
    loads[3].wait()
    pre_gate[...] = jnp.dot(x_full[...], wg[...], preferred_element_type=F32)
    pre_up[...] = jnp.dot(x_full[...], wu[...], preferred_element_type=F32)
    loads[4].wait()

    pass_on(send_c, recv_c, zc_s, zc_r, tc_s, tc_r)
    own_c.wait()
    from_peer(send_c, recv_c, tc_s, tc_r)
    assemble(recv_c, c_full)
    d_hidden = jnp.dot(c_full[...], wd[...], preferred_element_type=F32)
    sigma = jax.nn.sigmoid(pre_gate[...])
    activated = pre_gate[...] * sigma
    width = hidden.shape[1]
    hidden[...] = (activated * pre_up[...]).astype(BF16)
    d_both[:, :width] = (
        d_hidden * pre_up[...] * sigma * (1.0 + pre_gate[...] * (1.0 - sigma))
    ).astype(BF16)
    d_both[:, width:] = (d_hidden * activated).astype(BF16)

    over_rows = (((0,), (0,)), ((), ()))

    def weight_block(b, carry):
        col = pl.multiple_of(b * 256, 256)
        both = lax.dot_general(x_full[:, pl.ds(col, 256)], d_both[...], over_rows, preferred_element_type=F32)
        down = lax.dot_general(c_full[:, pl.ds(col, 256)], hidden[...], over_rows, preferred_element_type=F32)
        for m, value in enumerate((both[:, :width], both[:, width:], down)):
            value = value.astype(BF16)
            for k in range(NX):
                for q in range(4):
                    rows = value[k * 64 + q * 16 : k * 64 + q * 16 + 16, :]
                    if q < 2:
                        pa[b, q, k, m * 16 : m * 16 + 16, :] = rows
                    else:
                        pb[k, q - 2, b, m * 16 : m * 16 + 16, :] = rows
        return carry

    lax.fori_loop(0, NY, weight_block, 0)

    rings = {
        "a": (NY, y, at_y, pa, ra, ra_s, ra_r),
        "b": (NX, x, at_x, pb, rb, rb_s, rb_r),
        "a2": (NX, x, at_x, pa2, ra2, ra2_s, ra2_r),
        "b2": (NY, y, at_y, pb2, rb2, rb2_s, rb2_r),
    }

    def hop(ring, chain, h):
        n, me, at, parts, slots, send, recv = rings[ring]
        sign, part, length, base = chain
        target = lax.rem(me + n + sign, n)
        dest = lax.rem(me + n + sign * (length - h), n)
        src = parts.at[dest, part] if h == 0 else slots.at[base + h - 1]
        return pltpu.make_async_remote_copy(
            src_ref=src, dst_ref=slots.at[base + h], send_sem=send.at[base + h], recv_sem=recv.at[base + h],
            device_id=at(target), device_id_type=MESH,
        )

    def begin(ring):
        for chain in chains_of(rings[ring][0]):
            hop(ring, chain, 0).start()

    def serve(ring, which, h):
        n, me, at, parts, slots, send, recv = rings[ring]
        for chain in chains_of(n)[2 * which : 2 * which + 2]:
            sign, part, length, base = chain
            hop(ring, chain, h).wait_recv()
            if h < length - 1:
                dest = lax.rem(me + n + sign * (length - h - 1), n)

                def add(i, carry, base=base, h=h, dest=dest, part=part):
                    total = slots[base + h, i].astype(F32) + parts[dest, part, i].astype(F32)
                    slots[base + h, i] = total.astype(BF16)
                    return carry

                lax.fori_loop(0, parts.shape[2], add, 0)
                hop(ring, chain, h + 1).start()

    def finish(ring, store):
        n, me, at, parts, slots, send, recv = rings[ring]
        for part in range(2):
            last = [base + length - 1 for sign, p, length, base in chains_of(n) if p == part]

            def one(i, carry, part=part, last=last):
                store(
                    part, i,
                    parts[me, part, i].astype(F32) + slots[last[0], i].astype(F32) + slots[last[1], i].astype(F32),
                )
                return carry

            lax.fori_loop(0, parts.shape[2], one, 0)

    def to_a2(part, i, total):
        pa2[i, part, 0] = total.astype(BF16)

    def to_b2(part, i, total):
        pb2[i, part, 0] = total.astype(BF16)

    def to_out(first):
        def store(part, i, total):
            row = (first + part) * 16
            for m, out in enumerate((out_gate, out_up, out_down)):
                out[row : row + 16, :] = total[m * 16 : m * 16 + 16, :]

        return store

    begin("a")
    begin("b")

    over_width = (((1,), (1,)), ((), ()))

    def route_block(row):
        rows = pl.ds(pl.multiple_of(row, 256), 256)
        return lax.dot_general(
            d_both[:, :width], wg[rows, :], over_width, preferred_element_type=F32
        ) + lax.dot_general(d_both[:, width:], wu[rows, :], over_width, preferred_element_type=F32)

    def peer_copy(b):
        return pltpu.make_async_remote_copy(
            src_ref=peer_out.at[b], dst_ref=peer_in.at[b], send_sem=p_s.at[b], recv_sem=p_r.at[b],
            device_id=at_peer, device_id_type=MESH,
        )

    blocks = cols // 256

    def for_peer(b, carry):
        peer_out[b] = route_block(peer * cols + b * 256).astype(BF16)
        peer_copy(b).start()
        return carry

    def for_own(b, carry):
        own_part[b] = route_block(c * cols + b * 256)
        return carry

    lax.fori_loop(0, blocks, for_peer, 0)
    lax.fori_loop(0, blocks, for_own, 0)
    serve("a", 0, 0)

    def join(b, carry):
        peer_copy(b).wait_recv()
        total = (own_part[b] + peer_in[b].astype(F32))
        col = pl.multiple_of(b * 256, 256)
        for e in range(NZ):
            back_out[e, :, pl.ds(col, 256)] = total[e * CAP : (e + 1) * CAP, :].astype(BF16)
        return carry

    lax.fori_loop(0, blocks, join, 0)

    def back_copy(target, slab):
        return pltpu.make_async_remote_copy(
            src_ref=back_out.at[target], dst_ref=back_in.at[slab], send_sem=back_s.at[target],
            recv_sem=back_r.at[slab], device_id=at_z(target), device_id_type=MESH,
        )

    def send_back(i, carry):
        back_copy(turn(i), z).start()
        return carry

    lax.fori_loop(1, NZ, send_back, 0)
    own_back = pltpu.make_async_copy(back_out.at[z], back_in.at[z], loc_sem.at[2])
    own_back.start()

    serve("a", 1, 0)
    serve("b", 0, 0)
    serve("a", 0, 1)
    serve("a", 1, 1)
    serve("b", 1, 0)
    serve("a", 0, 2)
    serve("a", 1, 2)
    serve("b", 0, 1)
    finish("b", to_b2)
    begin("b2")
    serve("a", 0, 3)
    finish("a", to_a2)
    begin("a2")
    serve("b2", 0, 0)
    serve("b2", 1, 0)
    serve("a2", 0, 0)
    serve("a2", 1, 0)
    serve("b2", 0, 1)
    serve("b2", 1, 1)
    serve("a2", 0, 1)
    finish("a2", to_out(0))
    serve("b2", 0, 2)
    serve("b2", 1, 2)
    serve("b2", 0, 3)
    finish("b2", to_out(2))

    def arrived(i, carry):
        back_copy(turn(i), turn(i)).wait_recv()
        return carry

    lax.fori_loop(1, NZ, arrived, 0)
    own_back.wait()

    def token_block(b, carry):
        col = pl.multiple_of(b * 256, 256)
        rows = [back_in[e, :, pl.ds(col, 256)].astype(F32) for e in range(NZ)]
        rows = jnp.concatenate(rows, axis=0).astype(BF16)
        out_tok[:, pl.ds(col, 256)] = lax.dot_general(
            place[...], rows, over_rows, preferred_element_type=F32
        ).astype(BF16)
        return carry

    lax.fori_loop(0, blocks, token_block, 0)

    def sent(i, carry):
        target = turn(i)
        z_copy(send_x, recv_x, zx_s, zx_r, target, z).wait_send()
        z_copy(send_c, recv_c, zc_s, zc_r, target, z).wait_send()
        back_copy(target, z).wait_send()
        return carry

    lax.fori_loop(1, NZ, sent, 0)

    def sent_peer(i, carry):
        t_copy(send_x.at[i], recv_x, c, tx_s, tx_r, i).wait_send()
        t_copy(send_c.at[i], recv_c, c, tc_s, tc_r, i).wait_send()
        return carry

    lax.fori_loop(0, NZ, sent_peer, 0)

    def sent_blocks(b, carry):
        peer_copy(b).wait_send()
        return carry

    lax.fori_loop(0, blocks, sent_blocks, 0)
    for ring in rings:
        for chain in chains_of(rings[ring][0]):
            for h in range(chain[2]):
                hop(ring, chain, h).wait_send()


def per_device(tokens, cotangent, route_ids, gate_codes, w_gate, w_up, w_down):
    rows, cols = tokens.shape
    depth, width = w_gate.shape[1:]
    dma = lambda n: pltpu.SemaphoreType.DMA((n,))
    vm = pltpu.VMEM
    a_hops, b_hops = NY - 1, NX - 1
    scratch = [
        vm((rows, cols), BF16), vm((rows, cols), BF16),
        vm((depth, width), BF16), vm((depth, width), BF16), vm((depth, width), BF16),
        vm((SLOTS, rows), BF16),
        vm((NZ, CAP, cols), BF16), vm((NZ, CAP, cols), BF16),
        vm((2, NZ, CAP, cols), BF16), vm((2, NZ, CAP, cols), BF16),
        vm((SLOTS, depth), BF16), vm((SLOTS, depth), BF16),
        vm((SLOTS, width), F32), vm((SLOTS, width), F32),
        vm((SLOTS, 2 * width), BF16), vm((SLOTS, width), BF16),
        vm((cols // 256, SLOTS, 256), F32), vm((cols // 256, SLOTS, 256), BF16), vm((cols // 256, SLOTS, 256), BF16),
        vm((NZ, CAP, cols), BF16), vm((NZ, CAP, cols), BF16),
        vm((NY, 2, NX, 48, width), BF16), vm((NX, 2, NY, 48, width), BF16),
        vm((NX, 2, 1, 48, width), BF16), vm((NY, 2, 1, 48, width), BF16),
        vm((2 * a_hops, NX, 48, width), BF16), vm((2 * b_hops, NY, 48, width), BF16),
        vm((2 * b_hops, 1, 48, width), BF16), vm((2 * a_hops, 1, 48, width), BF16),
        dma(5), dma(NZ), dma(NZ), dma(NZ), dma(NZ), dma(NZ), dma(NZ), dma(NZ), dma(NZ), dma(3),
        dma(4), dma(4), dma(NZ), dma(NZ),
        dma(2 * a_hops), dma(2 * a_hops), dma(2 * b_hops), dma(2 * b_hops),
        dma(2 * b_hops), dma(2 * b_hops), dma(2 * a_hops), dma(2 * a_hops),
    ]
    in_vmem = pl.BlockSpec(memory_space=pltpu.VMEM)
    anywhere = pl.BlockSpec(memory_space=pl.ANY)
    out_rows = depth // (NX * NY)
    weight_out = jax.ShapeDtypeStruct((out_rows, width), F32)
    token_grad, grad_gate, grad_up, grad_down = pl.pallas_call(
        kernel,
        out_shape=(jax.ShapeDtypeStruct((rows, cols), BF16), weight_out, weight_out, weight_out),
        in_specs=[in_vmem, in_vmem] + [anywhere] * 5,
        out_specs=(in_vmem,) * 4,
        scratch_shapes=scratch,
        compiler_params=pltpu.CompilerParams(
            collective_id=0, has_side_effects=True, vmem_limit_bytes=56 * 1024 * 1024
        ),
        name="moe_backward",
    )(route_ids.T, gate_codes.T, tokens, cotangent, w_gate[0], w_up[0], w_down[0])
    return token_grad, grad_gate[None], grad_up[None], grad_down[None]


def solution(mesh):
    in_specs = (
        P(("dp", "expert"), "tensor"),
        P(("dp", "expert"), "tensor"),
        P(("dp", "expert"), None),
        P(("dp", "expert"), None),
        P("expert", None, "tensor"),
        P("expert", None, "tensor"),
        P("expert", None, "tensor"),
    )
    out_specs = (
        P(("dp", "expert"), "tensor"),
        P("expert", "dp", "tensor"),
        P("expert", "dp", "tensor"),
        P("expert", "dp", "tensor"),
    )
    return jax.shard_map(
        per_device, mesh=mesh, in_specs=in_specs, out_specs=out_specs, check_vma=False
    )
```

```python
import functools

import jax
import jax.numpy as jnp
from jax import lax
from jax.experimental import pallas as pl
from jax.experimental.pallas import tpu as pltpu
from jax.sharding import PartitionSpec as P

MESH = pl.DeviceIdType.MESH
F32 = jnp.float32
BF16 = jnp.bfloat16
NX, NY, NZ = 4, 8, 12
CAP = 24
SLOTS = NZ * CAP
GATE_UNIT = 65536.0


Y_ORDER = (4, 3, -3, 2, -2, 1, -1, 0)
X_ORDER = (2, 1, -1, 0)
A_UNITS = (((0, 0), (0, 1), (0, 2)), ((1, 0), (1, 1)))
B_UNITS = (((2, 0), (2, 1), (2, 2)), ((3, 0), (3, 1), (3, 2), (1, 2)))


def chains_of(n):
    half = n // 2
    return ((1, 0, half), (-1, 1, half), (1, 1, half - 1), (-1, 0, half - 1))


def kernel(
    ids_ref, codes_ref, tok_hbm, cot_hbm, wg_hbm, wu_hbm, wd_hbm,
    out_tok, out_gate, out_up, out_down,
    tok, cot, wg, wu, wd, place, send_x, send_c, recv_x, recv_c, x_full, c_full, pre_gate, pre_up,
    d_both, hidden, own_part, peer_out, peer_in, back_out, back_in, tok_grad,
    parts_a, parts_b, parts_a2, parts_b2, slots_a, slots_b, slots_a2, slots_b2,
    in_sem, zx_s, zx_r, zc_s, zc_r, tx_s, tx_r, tc_s, tc_r, loc_sem, p_s, p_r, back_s, back_r,
    ra_s, ra_r, rb_s, rb_r, ra2_s, ra2_r, rb2_s, rb2_r,
):
    dp = lax.axis_index("dp")
    z = lax.axis_index("expert")
    c = lax.axis_index("tensor")
    y, x = dp // NX, dp % NX
    peer = 1 - c
    cols = tok.shape[1]

    loads = [
        pltpu.make_async_copy(src, dst, in_sem.at[i])
        for i, (src, dst) in enumerate(((tok_hbm, tok), (cot_hbm, cot), (wg_hbm, wg), (wu_hbm, wu), (wd_hbm, wd)))
    ]
    for load in loads:
        load.start()

    def at_z(k):
        return (dp, k, c)

    def at_x(k):
        return (y * NX + k, z, c)

    def at_y(k):
        return (k * NX + x, z, c)

    at_peer = (dp, z, peer)

    barrier = pltpu.get_barrier_semaphore()

    def greet(i, carry):
        pl.semaphore_signal(barrier, inc=1, device_id=at_z(lax.rem(z + i, NZ)), device_id_type=MESH)
        return carry

    lax.fori_loop(1, NZ, greet, 0)
    pl.semaphore_signal(barrier, inc=1, device_id=at_peer, device_id_type=MESH)
    for step in (1, NX - 1):
        pl.semaphore_signal(barrier, inc=1, device_id=at_x(lax.rem(x + step, NX)), device_id_type=MESH)
    for step in (1, NY - 1):
        pl.semaphore_signal(barrier, inc=1, device_id=at_y(lax.rem(y + step, NY)), device_id_type=MESH)

    count = ids_ref.shape[1]
    expert_row = lax.broadcasted_iota(jnp.int32, (16, count), 0)
    match = jnp.zeros((16, count), F32)
    gates = jnp.zeros((16, count), F32)
    for k in range(ids_ref.shape[0]):
        same = ids_ref[k : k + 1, :] == expert_row
        match = match + jnp.where(same, 1.0, 0.0)
        gates = gates + jnp.where(same, codes_ref[k : k + 1, :].astype(F32) / GATE_UNIT, 0.0)
    before = jnp.where(
        lax.broadcasted_iota(jnp.int32, (count, count), 0) < lax.broadcasted_iota(jnp.int32, (count, count), 1),
        1.0, 0.0,
    ).astype(BF16)
    position = jnp.dot(match.astype(BF16), before, preferred_element_type=F32)
    position = jnp.where(match > 0.5, position, -1.0)
    slot_row = lax.broadcasted_iota(jnp.int32, (CAP, count), 0).astype(F32)
    pieces, slot_gates = [], []
    for e in range(NZ):
        piece = jnp.where(position[e : e + 1, :] == slot_row, 1.0, 0.0)
        pieces.append(piece)
        slot_gates.append(jnp.sum(piece * gates[e : e + 1, :], axis=1, keepdims=True))
    place[...] = jnp.concatenate(pieces, axis=0).astype(BF16)
    slot_gate = jnp.concatenate(slot_gates, axis=0)

    def z_copy(src, dst, send, recv, target, slab):
        return pltpu.make_async_remote_copy(
            src_ref=src.at[target], dst_ref=dst.at[c, slab], send_sem=send.at[target], recv_sem=recv.at[slab],
            device_id=at_z(target), device_id_type=MESH,
        )

    def t_copy(src, dst, half, send, recv, slab):
        return pltpu.make_async_remote_copy(
            src_ref=src, dst_ref=dst.at[half, slab], send_sem=send.at[slab], recv_sem=recv.at[slab],
            device_id=at_peer, device_id_type=MESH,
        )

    def turn(i):
        step = (i + 1) // 2
        return lax.rem(z + NZ + jnp.where(i % 2 == 1, step, -step), NZ)

    def gather(table, buffer, scale):
        for block in range(cols // 256):
            part = jnp.dot(place[...], table[:, block * 256 : block * 256 + 256], preferred_element_type=F32)
            if scale is not None:
                part = scale * part
            for e in range(NZ):
                buffer[e, :, block * 256 : block * 256 + 256] = part[e * CAP : (e + 1) * CAP, :].astype(BF16)

    def send_all(src, dst, zs, zr, ts, tr, own):
        def one(i, carry):
            z_copy(src, dst, zs, zr, turn(i), z).start()
            return carry

        lax.fori_loop(1, NZ, one, 0)
        t_copy(src.at[z], dst, c, ts, tr, z).start()
        own_copy = pltpu.make_async_copy(src.at[z], dst.at[c, z], loc_sem.at[own])
        own_copy.start()
        return own_copy

    loads[0].wait()
    gather(tok, send_x, None)
    pl.semaphore_wait(barrier, NZ - 1 + 5)
    own_x = send_all(send_x, recv_x, zx_s, zx_r, tx_s, tx_r, 0)
    loads[1].wait()
    gather(cot, send_c, slot_gate)
    own_c = send_all(send_c, recv_c, zc_s, zc_r, tc_s, tc_r, 1)

    def pass_on(src, dst, zs, zr, ts, tr):
        def one(i, carry):
            slab = turn(i)
            z_copy(src, dst, zs, zr, slab, slab).wait_recv()
            t_copy(dst.at[c, slab], dst, c, ts, tr, slab).start()
            return carry

        lax.fori_loop(1, NZ, one, 0)

    def from_peer(src, dst, ts, tr):
        def one(i, carry):
            t_copy(src.at[i], dst, peer, ts, tr, i).wait_recv()
            return carry

        lax.fori_loop(0, NZ, one, 0)

    def assemble(slabs, full, half):
        def one(b, carry):
            col = pl.multiple_of(b * 256, 256)
            rows = [slabs[half, e, :, pl.ds(col, 256)].astype(F32) for e in range(NZ)]
            full[half, :, pl.ds(col, 256)] = jnp.concatenate(rows, axis=0).astype(BF16)
            return carry

        lax.fori_loop(0, cols // 256, one, 0)

    def product(full, weights, half):
        rows = pl.ds(pl.multiple_of(half * cols, cols), cols)
        return jnp.dot(full[half], weights[rows, :], preferred_element_type=F32)

    pass_on(send_x, recv_x, zx_s, zx_r, tx_s, tx_r)
    own_x.wait()
    from_peer(send_x, recv_x, tx_s, tx_r)
    loads[2].wait()
    loads[3].wait()
    assemble(recv_x, x_full, 0)
    assemble(recv_x, x_full, 1)
    pre_gate[...] = product(x_full, wg, 0)
    pre_gate[...] += product(x_full, wg, 1)
    pre_up[...] = product(x_full, wu, 0)
    pre_up[...] += product(x_full, wu, 1)
    loads[4].wait()

    pass_on(send_c, recv_c, zc_s, zc_r, tc_s, tc_r)
    own_c.wait()
    assemble(recv_c, c_full, c)
    d_own = product(c_full, wd, c)
    from_peer(send_c, recv_c, tc_s, tc_r)
    assemble(recv_c, c_full, peer)
    d_hidden = d_own + product(c_full, wd, peer)
    sigma = jax.nn.sigmoid(pre_gate[...])
    activated = pre_gate[...] * sigma
    width = hidden.shape[1]
    hidden[...] = (activated * pre_up[...]).astype(BF16)
    d_both[:, :width] = (
        d_hidden * pre_up[...] * sigma * (1.0 + pre_gate[...] * (1.0 - sigma))
    ).astype(BF16)
    d_both[:, width:] = (d_hidden * activated).astype(BF16)

    over_rows = (((0,), (0,)), ((), ()))

    def x_place(k):
        gap = lax.rem(k - x + NX, NX)
        return jnp.where(gap == 0, 3, jnp.where(gap == 1, 1, jnp.where(gap == 2, 0, 2)))

    x_places = [x_place(k) for k in range(NX)]

    def weight_block(j, carry):
        offset = jnp.where(j % 2 == 0, -((NY - j) // 2), (NY - 1 - j) // 2)
        b = lax.rem(y + offset + NY, NY)
        side = b // (NY // 2)
        col = pl.multiple_of(lax.rem(b, NY // 2) * 256, 256)
        both = lax.dot_general(
            x_full[side, :, pl.ds(col, 256)], d_both[...], over_rows, preferred_element_type=F32
        )
        down = lax.dot_general(
            c_full[side, :, pl.ds(col, 256)], hidden[...], over_rows, preferred_element_type=F32
        )
        values = [v.astype(BF16) for v in (both[:, :width], both[:, width:], down)]
        for k in range(NX):
            for p in range(2):
                for u, (q, m) in enumerate(A_UNITS[p]):
                    row = k * 64 + q * 16
                    parts_a[p][b, x_places[k], u * 16 : u * 16 + 16, :] = values[m][row : row + 16, :]
                for u, (q, m) in enumerate(B_UNITS[p]):
                    row = k * 64 + q * 16
                    parts_b[p][k, j, u * 16 : u * 16 + 16, :] = values[m][row : row + 16, :]
        return carry

    rings = {
        "a": (NY, y, at_y, parts_a, slots_a, ra_s, ra_r, 2, 2),
        "b": (NX, x, at_x, parts_b, slots_b, rb_s, rb_r, 4, 2),
        "a2": (NX, x, at_x, parts_a2, slots_a2, ra2_s, ra2_r, 1, 1),
        "b2": (NY, y, at_y, parts_b2, slots_b2, rb2_s, rb2_r, 1, 1),
    }

    def hop(ring, i, h, g):
        n, me, at, parts, slots, send, recv, groups, size = rings[ring]
        sign, part, length = chains_of(n)[i]
        target = lax.rem(me + n + sign, n)
        dest = lax.rem(me + n + sign * (length - h), n)
        piece = pl.ds(g * size, size)
        src = parts[part].at[dest, piece] if h == 0 else slots[i].at[h - 1, piece]
        sem = (sum(l for _, _, l in chains_of(n)[:i]) + h) * groups + g
        return pltpu.make_async_remote_copy(
            src_ref=src, dst_ref=slots[i].at[h, piece], send_sem=send.at[sem], recv_sem=recv.at[sem],
            device_id=at(target), device_id_type=MESH,
        )

    def begin(ring, which, g):
        for i in which:
            hop(ring, i, 0, g).start()

    def serve(ring, which, h, g):
        n, me, at, parts, slots, send, recv, groups, size = rings[ring]
        for i in which:
            sign, part, length = chains_of(n)[i]
            hop(ring, i, h, g).wait_recv()
            if h < length - 1:
                dest = lax.rem(me + n + sign * (length - h - 1), n)
                for k in range(g * size, g * size + size):
                    total = slots[i][h, k].astype(F32) + parts[part][dest, k].astype(F32)
                    slots[i][h, k] = total.astype(BF16)
                hop(ring, i, h + 1, g).start()

    def finish(ring, g, store):
        n, me, at, parts, slots, send, recv, groups, size = rings[ring]
        for part in range(2):
            ends = [(i, l - 1) for i, (_, p, l) in enumerate(chains_of(n)) if p == part]
            for k in range(g * size, g * size + size):
                total = parts[part][me, k].astype(F32)
                for i, h in ends:
                    total = total + slots[i][h, k].astype(F32)
                store(part, k, total)

    def to_a2(part, k, total):
        parts_a2[part][lax.rem(x + NX + X_ORDER[k], NX), 0] = total.astype(BF16)

    def to_b2(part, k, total):
        parts_b2[part][lax.rem(y + NY + Y_ORDER[k], NY), 0] = total.astype(BF16)

    def to_out(units):
        def store(part, k, total):
            for u, (q, m) in enumerate(units[part]):
                out = (out_gate, out_up, out_down)[m]
                out[q * 16 : q * 16 + 16, :] = total[u * 16 : u * 16 + 16, :]

        return store

    every, long, short = (0, 1, 2, 3), (0, 1), (2, 3)
    lax.fori_loop(0, 2, weight_block, 0)
    for g in range(2):
        begin("a", long, g)
    for g in range(2):
        begin("a", (2,), g)
    begin("b", every, 0)
    lax.fori_loop(2, 4, weight_block, 0)
    for g in range(2):
        begin("a", (3,), g)
    begin("b", every, 1)
    lax.fori_loop(4, NY, weight_block, 0)

    over_width = (((1,), (1,)), ((), ()))

    def route_block(row):
        rows = pl.ds(pl.multiple_of(row, 256), 256)
        return lax.dot_general(
            d_both[:, :width], wg[rows, :], over_width, preferred_element_type=F32
        ) + lax.dot_general(d_both[:, width:], wu[rows, :], over_width, preferred_element_type=F32)

    def peer_copy(b):
        return pltpu.make_async_remote_copy(
            src_ref=peer_out.at[b], dst_ref=peer_in.at[b], send_sem=p_s.at[b], recv_sem=p_r.at[b],
            device_id=at_peer, device_id_type=MESH,
        )

    blocks = cols // 256

    def for_peer(b, carry):
        peer_out[b] = route_block(peer * cols + b * 256).astype(BF16)
        peer_copy(b).start()
        return carry

    def for_own(b, carry):
        own_part[b] = route_block(c * cols + b * 256)
        return carry

    lax.fori_loop(0, blocks, for_peer, 0)
    lax.fori_loop(0, blocks, for_own, 0)
    serve("a", long, 0, 0)
    serve("a", long, 0, 1)

    def join(b, carry):
        peer_copy(b).wait_recv()
        total = (own_part[b] + peer_in[b].astype(F32))
        col = pl.multiple_of(b * 256, 256)
        for e in range(NZ):
            back_out[e, :, pl.ds(col, 256)] = total[e * CAP : (e + 1) * CAP, :].astype(BF16)
        return carry

    lax.fori_loop(0, blocks, join, 0)

    def back_copy(target, slab):
        return pltpu.make_async_remote_copy(
            src_ref=back_out.at[target], dst_ref=back_in.at[slab], send_sem=back_s.at[target],
            recv_sem=back_r.at[slab], device_id=at_z(target), device_id_type=MESH,
        )

    def send_back(i, carry):
        back_copy(turn(i), z).start()
        return carry

    lax.fori_loop(1, NZ, send_back, 0)
    own_back = pltpu.make_async_copy(back_out.at[z], back_in.at[z], loc_sem.at[2])
    own_back.start()

    serve("a", short, 0, 0)
    serve("b", long, 0, 0)
    begin("b", every, 2)
    serve("a", short, 0, 1)
    serve("a", long, 1, 0)
    serve("b", short, 0, 0)
    serve("b", long, 1, 0)
    finish("b", 0, to_b2)
    begin("b2", (0, 1, 2), 0)
    serve("a", long, 1, 1)
    serve("b", long, 0, 1)
    begin("b", every, 3)
    serve("a", short, 1, 0)
    serve("a", short, 1, 1)
    serve("a", long, 2, 0)
    serve("b", short, 0, 1)
    serve("b", long, 1, 1)
    finish("b", 1, to_b2)
    begin("b2", (3,), 0)
    serve("b2", (0, 1, 2), 0, 0)
    serve("a", long, 2, 1)
    serve("b", long, 0, 2)
    serve("a", short, 2, 0)
    serve("a", short, 2, 1)
    serve("b2", (0,), 1, 0)
    serve("b", short, 0, 2)
    serve("b", long, 1, 2)
    finish("b", 2, to_b2)
    serve("b2", (3,), 0, 0)
    serve("b2", (1, 2), 1, 0)
    serve("b2", (0,), 2, 0)
    serve("b", long, 0, 3)
    serve("a", long, 3, 0)
    finish("a", 0, to_a2)
    begin("a2", (0, 1, 2), 0)
    serve("a", long, 3, 1)
    finish("a", 1, to_a2)
    begin("a2", (3,), 0)
    serve("b", short, 0, 3)
    serve("b", long, 1, 3)
    finish("b", 3, to_b2)
    serve("b2", (1,), 2, 0)
    serve("b2", (3,), 1, 0)
    serve("a2", long, 0, 0)

    def arrived(i, carry):
        back_copy(turn(i), turn(i)).wait_recv()
        return carry

    lax.fori_loop(1, NZ, arrived, 0)
    own_back.wait()

    def token_block(b, carry):
        col = pl.multiple_of(b * 256, 256)
        rows = [back_in[e, :, pl.ds(col, 256)].astype(F32) for e in range(NZ)]
        rows = jnp.concatenate(rows, axis=0).astype(BF16)
        tok_grad[:, pl.ds(col, 256)] = lax.dot_general(
            place[...], rows, over_rows, preferred_element_type=F32
        ).astype(BF16)
        return carry

    lax.fori_loop(0, blocks, token_block, 0)
    tok_out = pltpu.make_async_copy(tok_grad, out_tok, loc_sem.at[3])
    tok_out.start()

    serve("a2", short, 0, 0)
    serve("a2", long, 1, 0)
    finish("a2", 0, to_out(A_UNITS))
    serve("b2", (0, 1), 3, 0)
    serve("b2", (2, 3), 2, 0)
    finish("b2", 0, to_out(B_UNITS))
    tok_out.wait()

    def sent(i, carry):
        target = turn(i)
        z_copy(send_x, recv_x, zx_s, zx_r, target, z).wait_send()
        z_copy(send_c, recv_c, zc_s, zc_r, target, z).wait_send()
        back_copy(target, z).wait_send()
        return carry

    lax.fori_loop(1, NZ, sent, 0)

    def sent_peer(i, carry):
        t_copy(send_x.at[i], recv_x, c, tx_s, tx_r, i).wait_send()
        t_copy(send_c.at[i], recv_c, c, tc_s, tc_r, i).wait_send()
        return carry

    lax.fori_loop(0, NZ, sent_peer, 0)

    def sent_blocks(b, carry):
        peer_copy(b).wait_send()
        return carry

    lax.fori_loop(0, blocks, sent_blocks, 0)
    for ring in rings:
        n, groups = rings[ring][0], rings[ring][7]
        for i, chain in enumerate(chains_of(n)):
            for h in range(chain[2]):
                for g in range(groups):
                    hop(ring, i, h, g).wait_send()


def finish_kernel(a, b, c, d, out_a, out_b, out_c, out_d, held_a, held_b, held_c, held_d, in_sems, out_sems):
    sources, outs, held = (a, b, c, d), (out_a, out_b, out_c, out_d), (held_a, held_b, held_c, held_d)
    loads = [pltpu.make_async_copy(src, buf, in_sems.at[i]) for i, (src, buf) in enumerate(zip(sources, held))]
    stores = [pltpu.make_async_copy(buf, out, out_sems.at[i]) for i, (buf, out) in enumerate(zip(held, outs))]
    for load in loads:
        load.start()
    for load, store in zip(loads, stores):
        load.wait()
        store.start()
    for store in stores:
        store.wait()


def per_device(tokens, cotangent, route_ids, gate_codes, w_gate, w_up, w_down):
    rows, cols = tokens.shape
    depth, width = w_gate.shape[1:]
    dma = lambda n: pltpu.SemaphoreType.DMA((n,))
    vm = pltpu.VMEM
    a_hops, b_hops = NY - 1, NX - 1

    def parts_of(n, blocks, units):
        return [vm((n, blocks, 16 * len(u), width), BF16) for u in units]

    def slots_of(n, blocks, units):
        return [vm((length, blocks, 16 * len(units[part]), width), BF16) for _, part, length in chains_of(n)]

    scratch = [
        vm((rows, cols), BF16), vm((rows, cols), BF16),
        vm((depth, width), BF16), vm((depth, width), BF16), vm((depth, width), BF16),
        vm((SLOTS, rows), BF16),
        vm((NZ, CAP, cols), BF16), vm((NZ, CAP, cols), BF16),
        vm((2, NZ, CAP, cols), BF16), vm((2, NZ, CAP, cols), BF16),
        vm((2, SLOTS, cols), BF16), vm((2, SLOTS, cols), BF16),
        vm((SLOTS, width), F32), vm((SLOTS, width), F32),
        vm((SLOTS, 2 * width), BF16), vm((SLOTS, width), BF16),
        vm((cols // 256, SLOTS, 256), F32), vm((cols // 256, SLOTS, 256), BF16), vm((cols // 256, SLOTS, 256), BF16),
        vm((NZ, CAP, cols), BF16), vm((NZ, CAP, cols), BF16),
        vm((rows, cols), BF16),
        parts_of(NY, NX, A_UNITS), parts_of(NX, NY, B_UNITS), parts_of(NX, 1, A_UNITS), parts_of(NY, 1, B_UNITS),
        slots_of(NY, NX, A_UNITS), slots_of(NX, NY, B_UNITS), slots_of(NX, 1, A_UNITS), slots_of(NY, 1, B_UNITS),
        dma(5), dma(NZ), dma(NZ), dma(NZ), dma(NZ), dma(NZ), dma(NZ), dma(NZ), dma(NZ), dma(4),
        dma(4), dma(4), dma(NZ), dma(NZ),
        dma(4 * a_hops), dma(4 * a_hops), dma(8 * b_hops), dma(8 * b_hops),
        dma(2 * b_hops), dma(2 * b_hops), dma(2 * a_hops), dma(2 * a_hops),
    ]
    in_vmem = pl.BlockSpec(memory_space=pltpu.VMEM)
    anywhere = pl.BlockSpec(memory_space=pl.ANY)
    out_rows = depth // (NX * NY)
    weight_out = jax.ShapeDtypeStruct((out_rows, width), F32)
    results = (jax.ShapeDtypeStruct((rows, cols), BF16), weight_out, weight_out, weight_out)
    made = pl.pallas_call(
        kernel,
        out_shape=results,
        in_specs=[in_vmem, in_vmem] + [anywhere] * 5,
        out_specs=(anywhere, in_vmem, in_vmem, in_vmem),
        scratch_shapes=scratch,
        compiler_params=pltpu.CompilerParams(
            collective_id=0, has_side_effects=True, vmem_limit_bytes=56 * 1024 * 1024
        ),
        name="moe_backward",
    )(route_ids.T, gate_codes.T, tokens, cotangent, w_gate[0], w_up[0], w_down[0])
    token_grad, grad_gate, grad_up, grad_down = pl.pallas_call(
        finish_kernel,
        out_shape=results,
        in_specs=[anywhere] * 4,
        out_specs=(anywhere,) * 4,
        scratch_shapes=[vm(r.shape, r.dtype) for r in results] + [dma(4), dma(4)],
        name="moe_outputs",
    )(*made)
    return token_grad, grad_gate[None], grad_up[None], grad_down[None]


def solution(mesh):
    in_specs = (
        P(("dp", "expert"), "tensor"),
        P(("dp", "expert"), "tensor"),
        P(("dp", "expert"), None),
        P(("dp", "expert"), None),
        P("expert", None, "tensor"),
        P("expert", None, "tensor"),
        P("expert", None, "tensor"),
    )
    out_specs = (
        P(("dp", "expert"), "tensor"),
        P("expert", "dp", "tensor"),
        P("expert", "dp", "tensor"),
        P("expert", "dp", "tensor"),
    )
    return jax.shard_map(
        per_device, mesh=mesh, in_specs=in_specs, out_specs=out_specs, check_vma=False
    )
```

```python
import functools

import jax
import jax.numpy as jnp
from jax import lax
from jax.experimental import pallas as pl
from jax.experimental.pallas import tpu as pltpu
from jax.sharding import PartitionSpec as P

MESH = pl.DeviceIdType.MESH
F32 = jnp.float32
BF16 = jnp.bfloat16
NX, NY, NZ = 4, 8, 12
CAP = 24
SLOTS = NZ * CAP
GATE_UNIT = 65536.0


Y_ORDER = (4, 3, -3, 2, -2, 1, -1, 0)
X_ORDER = (2, 1, -1, 0)
A_UNITS = (((0, 0), (0, 1), (0, 2)), ((1, 0), (1, 1)))
B_UNITS = (((2, 0), (2, 1), (2, 2)), ((3, 0), (3, 1), (3, 2), (1, 2)))


def chains_of(n):
    half = n // 2
    return ((1, 0, half), (-1, 1, half), (1, 1, half - 1), (-1, 0, half - 1))


def kernel(
    ids_ref, codes_ref, tok_hbm, cot_hbm, wg_hbm, wu_hbm, wd_hbm,
    out_tok, out_gate, out_up, out_down,
    tok, cot, wg, wu, wd, place, send_x, send_c, recv_x, recv_c, x_full, c_full, to_gate, to_up,
    d_both, hidden, own_part, peer_out, peer_in, back_out, back_in, tok_grad,
    parts_a, parts_b, parts_a2, parts_b2, slots_a, slots_b, slots_a2, slots_b2,
    in_sem, zx_s, zx_r, zc_s, zc_r, tx_s, tx_r, tc_s, tc_r, loc_sem, p_s, p_r, back_s, back_r,
    ra_s, ra_r, rb_s, rb_r, ra2_s, ra2_r, rb2_s, rb2_r,
):
    dp = lax.axis_index("dp")
    z = lax.axis_index("expert")
    c = lax.axis_index("tensor")
    y, x = dp // NX, dp % NX
    peer = 1 - c
    cols = tok.shape[1]

    loads = [
        pltpu.make_async_copy(src, dst, in_sem.at[i])
        for i, (src, dst) in enumerate(((tok_hbm, tok), (cot_hbm, cot), (wg_hbm, wg), (wu_hbm, wu), (wd_hbm, wd)))
    ]
    for load in loads:
        load.start()

    def at_z(k):
        return (dp, k, c)

    def at_x(k):
        return (y * NX + k, z, c)

    def at_y(k):
        return (k * NX + x, z, c)

    at_peer = (dp, z, peer)

    barrier = pltpu.get_barrier_semaphore()

    def greet(i, carry):
        pl.semaphore_signal(barrier, inc=1, device_id=at_z(lax.rem(z + i, NZ)), device_id_type=MESH)
        return carry

    lax.fori_loop(1, NZ, greet, 0)
    pl.semaphore_signal(barrier, inc=1, device_id=at_peer, device_id_type=MESH)
    for step in (1, NX - 1):
        pl.semaphore_signal(barrier, inc=1, device_id=at_x(lax.rem(x + step, NX)), device_id_type=MESH)
    for step in (1, NY - 1):
        pl.semaphore_signal(barrier, inc=1, device_id=at_y(lax.rem(y + step, NY)), device_id_type=MESH)

    count = ids_ref.shape[1]
    expert_row = lax.broadcasted_iota(jnp.int32, (16, count), 0)
    match = jnp.zeros((16, count), F32)
    for k in range(ids_ref.shape[0]):
        same = ids_ref[k : k + 1, :] == expert_row
        match = match + jnp.where(same, 1.0, 0.0)
    before = jnp.where(
        lax.broadcasted_iota(jnp.int32, (count, count), 0) < lax.broadcasted_iota(jnp.int32, (count, count), 1),
        1.0, 0.0,
    ).astype(BF16)
    position = jnp.dot(match.astype(BF16), before, preferred_element_type=F32)
    position = jnp.where(match > 0.5, position, -1.0)
    slot_row = lax.broadcasted_iota(jnp.int32, (CAP, count), 0).astype(F32)
    pieces = [jnp.where(position[e : e + 1, :] == slot_row, 1.0, 0.0) for e in range(NZ)]
    place[...] = jnp.concatenate(pieces, axis=0).astype(BF16)

    def z_copy(src, dst, send, recv, target, slab):
        return pltpu.make_async_remote_copy(
            src_ref=src.at[target], dst_ref=dst.at[c, slab], send_sem=send.at[target], recv_sem=recv.at[slab],
            device_id=at_z(target), device_id_type=MESH,
        )

    def t_copy(src, dst, half, send, recv, slab):
        return pltpu.make_async_remote_copy(
            src_ref=src, dst_ref=dst.at[half, slab], send_sem=send.at[slab], recv_sem=recv.at[slab],
            device_id=at_peer, device_id_type=MESH,
        )

    def turn(i):
        step = (i + 1) // 2
        return lax.rem(z + NZ + jnp.where(i % 2 == 1, step, -step), NZ)

    def gather(table, buffer, scale):
        for block in range(cols // 256):
            part = jnp.dot(place[...], table[:, block * 256 : block * 256 + 256], preferred_element_type=F32)
            if scale is not None:
                part = scale * part
            for e in range(NZ):
                buffer[e, :, block * 256 : block * 256 + 256] = part[e * CAP : (e + 1) * CAP, :].astype(BF16)

    def send_all(src, dst, zs, zr, ts, tr, own):
        def one(i, carry):
            z_copy(src, dst, zs, zr, turn(i), z).start()
            return carry

        lax.fori_loop(1, NZ, one, 0)
        t_copy(src.at[z], dst, c, ts, tr, z).start()
        own_copy = pltpu.make_async_copy(src.at[z], dst.at[c, z], loc_sem.at[own])
        own_copy.start()
        return own_copy

    loads[0].wait()
    gather(tok, send_x, None)
    pl.semaphore_wait(barrier, NZ - 1 + 5)
    own_x = send_all(send_x, recv_x, zx_s, zx_r, tx_s, tx_r, 0)
    gates = jnp.zeros((16, count), F32)
    for k in range(ids_ref.shape[0]):
        same = ids_ref[k : k + 1, :] == expert_row
        gates = gates + jnp.where(same, codes_ref[k : k + 1, :].astype(F32) / GATE_UNIT, 0.0)
    slot_gate = jnp.concatenate(
        [
            jnp.sum(place[e * CAP : (e + 1) * CAP, :].astype(F32) * gates[e : e + 1, :], axis=1, keepdims=True)
            for e in range(NZ)
        ],
        axis=0,
    )
    loads[1].wait()
    gather(cot, send_c, slot_gate)
    own_c = send_all(send_c, recv_c, zc_s, zc_r, tc_s, tc_r, 1)

    def pass_on(src, dst, zs, zr, ts, tr):
        def one(i, carry):
            slab = turn(i)
            z_copy(src, dst, zs, zr, slab, slab).wait_recv()
            t_copy(dst.at[c, slab], dst, c, ts, tr, slab).start()
            return carry

        lax.fori_loop(1, NZ, one, 0)

    def from_peer(src, dst, ts, tr):
        def one(i, carry):
            t_copy(src.at[i], dst, peer, ts, tr, i).wait_recv()
            return carry

        lax.fori_loop(0, NZ, one, 0)

    def assemble(slabs, full, half):
        def one(b, carry):
            col = pl.multiple_of(b * 256, 256)
            rows = [slabs[half, e, :, pl.ds(col, 256)].astype(F32) for e in range(NZ)]
            full[half, :, pl.ds(col, 256)] = jnp.concatenate(rows, axis=0).astype(BF16)
            return carry

        lax.fori_loop(0, cols // 256, one, 0)

    def product(full, weights, half):
        rows = pl.ds(pl.multiple_of(half * cols, cols), cols)
        return jnp.dot(full[half], weights[rows, :], preferred_element_type=F32)

    pass_on(send_x, recv_x, zx_s, zx_r, tx_s, tx_r)
    own_x.wait()
    from_peer(send_x, recv_x, tx_s, tx_r)
    loads[2].wait()
    loads[3].wait()
    assemble(recv_x, x_full, 0)
    assemble(recv_x, x_full, 1)
    gate = product(x_full, wg, 0) + product(x_full, wg, 1)
    up = product(x_full, wu, 0) + product(x_full, wu, 1)
    width = hidden.shape[1]
    sigma = jax.nn.sigmoid(gate)
    activated = gate * sigma
    hidden[...] = (activated * up).astype(BF16)
    to_gate[...] = up * sigma * (1.0 + gate * (1.0 - sigma))
    to_up[...] = activated
    loads[4].wait()

    pass_on(send_c, recv_c, zc_s, zc_r, tc_s, tc_r)
    own_c.wait()
    assemble(recv_c, c_full, c)
    d_own = product(c_full, wd, c)
    from_peer(send_c, recv_c, tc_s, tc_r)
    assemble(recv_c, c_full, peer)
    d_hidden = d_own + product(c_full, wd, peer)
    d_both[:, :width] = (d_hidden * to_gate[...]).astype(BF16)
    d_both[:, width:] = (d_hidden * to_up[...]).astype(BF16)

    over_rows = (((0,), (0,)), ((), ()))

    def x_place(k):
        gap = lax.rem(k - x + NX, NX)
        return jnp.where(gap == 0, 3, jnp.where(gap == 1, 1, jnp.where(gap == 2, 0, 2)))

    x_places = [x_place(k) for k in range(NX)]

    def weight_block(j, carry):
        offset = jnp.where(j % 2 == 0, -((NY - j) // 2), (NY - 1 - j) // 2)
        b = lax.rem(y + offset + NY, NY)
        side = b // (NY // 2)
        col = pl.multiple_of(lax.rem(b, NY // 2) * 256, 256)
        both = lax.dot_general(
            x_full[side, :, pl.ds(col, 256)], d_both[...], over_rows, preferred_element_type=F32
        )
        down = lax.dot_general(
            c_full[side, :, pl.ds(col, 256)], hidden[...], over_rows, preferred_element_type=F32
        )
        values = [v.astype(BF16) for v in (both[:, :width], both[:, width:], down)]
        for k in range(NX):
            for p in range(2):
                for u, (q, m) in enumerate(A_UNITS[p]):
                    row = k * 64 + q * 16
                    parts_a[p][b, x_places[k], u * 16 : u * 16 + 16, :] = values[m][row : row + 16, :]
                for u, (q, m) in enumerate(B_UNITS[p]):
                    row = k * 64 + q * 16
                    parts_b[p][k, j, u * 16 : u * 16 + 16, :] = values[m][row : row + 16, :]
        return carry

    rings = {
        "a": (NY, y, at_y, parts_a, slots_a, ra_s, ra_r, 2, 2),
        "b": (NX, x, at_x, parts_b, slots_b, rb_s, rb_r, 4, 2),
        "a2": (NX, x, at_x, parts_a2, slots_a2, ra2_s, ra2_r, 1, 1),
        "b2": (NY, y, at_y, parts_b2, slots_b2, rb2_s, rb2_r, 1, 1),
    }

    def hop(ring, i, h, g):
        n, me, at, parts, slots, send, recv, groups, size = rings[ring]
        sign, part, length = chains_of(n)[i]
        target = lax.rem(me + n + sign, n)
        dest = lax.rem(me + n + sign * (length - h), n)
        piece = pl.ds(g * size, size)
        src = parts[part].at[dest, piece] if h == 0 else slots[i].at[h - 1, piece]
        sem = (sum(l for _, _, l in chains_of(n)[:i]) + h) * groups + g
        return pltpu.make_async_remote_copy(
            src_ref=src, dst_ref=slots[i].at[h, piece], send_sem=send.at[sem], recv_sem=recv.at[sem],
            device_id=at(target), device_id_type=MESH,
        )

    def begin(ring, which, g):
        for i in which:
            hop(ring, i, 0, g).start()

    def serve(ring, which, h, g):
        n, me, at, parts, slots, send, recv, groups, size = rings[ring]
        for i in which:
            sign, part, length = chains_of(n)[i]
            hop(ring, i, h, g).wait_recv()
            if h < length - 1:
                dest = lax.rem(me + n + sign * (length - h - 1), n)
                for k in range(g * size, g * size + size):
                    total = slots[i][h, k].astype(F32) + parts[part][dest, k].astype(F32)
                    slots[i][h, k] = total.astype(BF16)
                hop(ring, i, h + 1, g).start()

    def finish(ring, g, store):
        n, me, at, parts, slots, send, recv, groups, size = rings[ring]
        for part in range(2):
            ends = [(i, l - 1) for i, (_, p, l) in enumerate(chains_of(n)) if p == part]
            for k in range(g * size, g * size + size):
                total = parts[part][me, k].astype(F32)
                for i, h in ends:
                    total = total + slots[i][h, k].astype(F32)
                store(part, k, total)

    def to_a2(part, k, total):
        parts_a2[part][lax.rem(x + NX + X_ORDER[k], NX), 0] = total.astype(BF16)

    def to_b2(part, k, total):
        parts_b2[part][lax.rem(y + NY + Y_ORDER[k], NY), 0] = total.astype(BF16)

    def to_out(units):
        def store(part, k, total):
            for u, (q, m) in enumerate(units[part]):
                out = (out_gate, out_up, out_down)[m]
                out[q * 16 : q * 16 + 16, :] = total[u * 16 : u * 16 + 16, :]

        return store

    every, long, short = (0, 1, 2, 3), (0, 1), (2, 3)

    over_width = (((1,), (1,)), ((), ()))

    def route_block(row):
        rows = pl.ds(pl.multiple_of(row, 256), 256)
        return lax.dot_general(
            d_both[:, :width], wg[rows, :], over_width, preferred_element_type=F32
        ) + lax.dot_general(d_both[:, width:], wu[rows, :], over_width, preferred_element_type=F32)

    def peer_copy(b):
        return pltpu.make_async_remote_copy(
            src_ref=peer_out.at[b], dst_ref=peer_in.at[b], send_sem=p_s.at[b], recv_sem=p_r.at[b],
            device_id=at_peer, device_id_type=MESH,
        )

    blocks = cols // 256

    def for_peer(b, carry):
        peer_out[b] = route_block(peer * cols + b * 256).astype(BF16)
        peer_copy(b).start()
        return carry

    def for_own(b, carry):
        own_part[b] = route_block(c * cols + b * 256)
        return carry

    lax.fori_loop(0, 3, weight_block, 0)
    for which in (long, short):
        for g in range(2):
            begin("a", which, g)
    begin("b", every, 0)
    lax.fori_loop(0, blocks, for_peer, 0)
    lax.fori_loop(3, 5, weight_block, 0)
    begin("b", every, 1)
    lax.fori_loop(0, blocks, for_own, 0)
    serve("a", long, 0, 0)
    serve("a", long, 0, 1)

    def join(b, carry):
        peer_copy(b).wait_recv()
        total = (own_part[b] + peer_in[b].astype(F32))
        col = pl.multiple_of(b * 256, 256)
        for e in range(NZ):
            back_out[e, :, pl.ds(col, 256)] = total[e * CAP : (e + 1) * CAP, :].astype(BF16)
        return carry

    lax.fori_loop(0, blocks, join, 0)

    def back_copy(target, slab):
        return pltpu.make_async_remote_copy(
            src_ref=back_out.at[target], dst_ref=back_in.at[slab], send_sem=back_s.at[target],
            recv_sem=back_r.at[slab], device_id=at_z(target), device_id_type=MESH,
        )

    def send_back(i, carry):
        back_copy(turn(i), z).start()
        return carry

    lax.fori_loop(1, NZ, send_back, 0)
    own_back = pltpu.make_async_copy(back_out.at[z], back_in.at[z], loc_sem.at[2])
    own_back.start()
    lax.fori_loop(5, NY, weight_block, 0)

    serve("a", short, 0, 0)
    serve("b", long, 0, 0)
    begin("b", every, 2)
    serve("a", short, 0, 1)
    serve("a", long, 1, 0)
    serve("b", short, 0, 0)
    serve("b", long, 1, 0)
    finish("b", 0, to_b2)
    begin("b2", (0, 1, 2), 0)
    serve("a", long, 1, 1)
    serve("b", long, 0, 1)
    begin("b", every, 3)
    serve("a", short, 1, 0)
    serve("a", short, 1, 1)
    serve("a", long, 2, 0)
    serve("b", short, 0, 1)
    serve("b", long, 1, 1)
    finish("b", 1, to_b2)
    begin("b2", (3,), 0)
    serve("b2", (0, 1, 2), 0, 0)
    serve("a", long, 2, 1)
    serve("b", long, 0, 2)
    serve("a", short, 2, 0)
    serve("a", short, 2, 1)
    serve("b2", (0,), 1, 0)
    serve("b", short, 0, 2)
    serve("b", long, 1, 2)
    finish("b", 2, to_b2)
    serve("b2", (3,), 0, 0)
    serve("b2", (1, 2), 1, 0)
    serve("b2", (0,), 2, 0)
    serve("b", long, 0, 3)
    serve("a", long, 3, 0)
    finish("a", 0, to_a2)
    begin("a2", (0, 1, 2), 0)
    serve("a", long, 3, 1)
    finish("a", 1, to_a2)
    begin("a2", (3,), 0)
    serve("b", short, 0, 3)
    serve("b", long, 1, 3)
    finish("b", 3, to_b2)
    serve("b2", (1,), 2, 0)
    serve("b2", (3,), 1, 0)
    serve("a2", long, 0, 0)

    def arrived(i, carry):
        back_copy(turn(i), turn(i)).wait_recv()
        return carry

    lax.fori_loop(1, NZ, arrived, 0)
    own_back.wait()

    def token_block(b, carry):
        col = pl.multiple_of(b * 256, 256)
        rows = [back_in[e, :, pl.ds(col, 256)].astype(F32) for e in range(NZ)]
        rows = jnp.concatenate(rows, axis=0).astype(BF16)
        tok_grad[:, pl.ds(col, 256)] = lax.dot_general(
            place[...], rows, over_rows, preferred_element_type=F32
        ).astype(BF16)
        return carry

    lax.fori_loop(0, blocks, token_block, 0)
    tok_out = pltpu.make_async_copy(tok_grad, out_tok, loc_sem.at[3])
    tok_out.start()

    serve("a2", short, 0, 0)
    serve("a2", long, 1, 0)
    finish("a2", 0, to_out(A_UNITS))
    serve("b2", (0, 1), 3, 0)
    serve("b2", (2, 3), 2, 0)
    finish("b2", 0, to_out(B_UNITS))
    tok_out.wait()

    def sent(i, carry):
        target = turn(i)
        z_copy(send_x, recv_x, zx_s, zx_r, target, z).wait_send()
        z_copy(send_c, recv_c, zc_s, zc_r, target, z).wait_send()
        back_copy(target, z).wait_send()
        return carry

    lax.fori_loop(1, NZ, sent, 0)

    def sent_peer(i, carry):
        t_copy(send_x.at[i], recv_x, c, tx_s, tx_r, i).wait_send()
        t_copy(send_c.at[i], recv_c, c, tc_s, tc_r, i).wait_send()
        return carry

    lax.fori_loop(0, NZ, sent_peer, 0)

    def sent_blocks(b, carry):
        peer_copy(b).wait_send()
        return carry

    lax.fori_loop(0, blocks, sent_blocks, 0)
    for ring in rings:
        n, groups = rings[ring][0], rings[ring][7]
        for i, chain in enumerate(chains_of(n)):
            for h in range(chain[2]):
                for g in range(groups):
                    hop(ring, i, h, g).wait_send()


def finish_kernel(a, b, c, d, out_a, out_b, out_c, out_d, held_a, held_b, held_c, held_d, in_sems, out_sems):
    sources, outs, held = (a, b, c, d), (out_a, out_b, out_c, out_d), (held_a, held_b, held_c, held_d)
    loads = [pltpu.make_async_copy(src, buf, in_sems.at[i]) for i, (src, buf) in enumerate(zip(sources, held))]
    stores = [pltpu.make_async_copy(buf, out, out_sems.at[i]) for i, (buf, out) in enumerate(zip(held, outs))]
    for load in loads:
        load.start()
    for load, store in zip(loads, stores):
        load.wait()
        store.start()
    for store in stores:
        store.wait()


def per_device(tokens, cotangent, route_ids, gate_codes, w_gate, w_up, w_down):
    rows, cols = tokens.shape
    depth, width = w_gate.shape[1:]
    dma = lambda n: pltpu.SemaphoreType.DMA((n,))
    vm = pltpu.VMEM
    a_hops, b_hops = NY - 1, NX - 1

    def parts_of(n, blocks, units):
        return [vm((n, blocks, 16 * len(u), width), BF16) for u in units]

    def slots_of(n, blocks, units):
        return [vm((length, blocks, 16 * len(units[part]), width), BF16) for _, part, length in chains_of(n)]

    scratch = [
        vm((rows, cols), BF16), vm((rows, cols), BF16),
        vm((depth, width), BF16), vm((depth, width), BF16), vm((depth, width), BF16),
        vm((SLOTS, rows), BF16),
        vm((NZ, CAP, cols), BF16), vm((NZ, CAP, cols), BF16),
        vm((2, NZ, CAP, cols), BF16), vm((2, NZ, CAP, cols), BF16),
        vm((2, SLOTS, cols), BF16), vm((2, SLOTS, cols), BF16),
        vm((SLOTS, width), F32), vm((SLOTS, width), F32),
        vm((SLOTS, 2 * width), BF16), vm((SLOTS, width), BF16),
        vm((cols // 256, SLOTS, 256), F32), vm((cols // 256, SLOTS, 256), BF16), vm((cols // 256, SLOTS, 256), BF16),
        vm((NZ, CAP, cols), BF16), vm((NZ, CAP, cols), BF16),
        vm((rows, cols), BF16),
        parts_of(NY, NX, A_UNITS), parts_of(NX, NY, B_UNITS), parts_of(NX, 1, A_UNITS), parts_of(NY, 1, B_UNITS),
        slots_of(NY, NX, A_UNITS), slots_of(NX, NY, B_UNITS), slots_of(NX, 1, A_UNITS), slots_of(NY, 1, B_UNITS),
        dma(5), dma(NZ), dma(NZ), dma(NZ), dma(NZ), dma(NZ), dma(NZ), dma(NZ), dma(NZ), dma(4),
        dma(4), dma(4), dma(NZ), dma(NZ),
        dma(4 * a_hops), dma(4 * a_hops), dma(8 * b_hops), dma(8 * b_hops),
        dma(2 * b_hops), dma(2 * b_hops), dma(2 * a_hops), dma(2 * a_hops),
    ]
    in_vmem = pl.BlockSpec(memory_space=pltpu.VMEM)
    anywhere = pl.BlockSpec(memory_space=pl.ANY)
    out_rows = depth // (NX * NY)
    weight_out = jax.ShapeDtypeStruct((out_rows, width), F32)
    results = (jax.ShapeDtypeStruct((rows, cols), BF16), weight_out, weight_out, weight_out)
    made = pl.pallas_call(
        kernel,
        out_shape=results,
        in_specs=[in_vmem, in_vmem] + [anywhere] * 5,
        out_specs=(anywhere, in_vmem, in_vmem, in_vmem),
        scratch_shapes=scratch,
        compiler_params=pltpu.CompilerParams(
            collective_id=0, has_side_effects=True, vmem_limit_bytes=56 * 1024 * 1024
        ),
        name="moe_backward",
    )(route_ids.T, gate_codes.T, tokens, cotangent, w_gate[0], w_up[0], w_down[0])
    token_grad, grad_gate, grad_up, grad_down = pl.pallas_call(
        finish_kernel,
        out_shape=results,
        in_specs=[anywhere] * 4,
        out_specs=(anywhere,) * 4,
        scratch_shapes=[vm(r.shape, r.dtype) for r in results] + [dma(4), dma(4)],
        name="moe_outputs",
    )(*made)
    return token_grad, grad_gate[None], grad_up[None], grad_down[None]


def solution(mesh):
    in_specs = (
        P(("dp", "expert"), "tensor"),
        P(("dp", "expert"), "tensor"),
        P(("dp", "expert"), None),
        P(("dp", "expert"), None),
        P("expert", None, "tensor"),
        P("expert", None, "tensor"),
        P("expert", None, "tensor"),
    )
    out_specs = (
        P(("dp", "expert"), "tensor"),
        P("expert", "dp", "tensor"),
        P("expert", "dp", "tensor"),
        P("expert", "dp", "tensor"),
    )
    return jax.shard_map(
        per_device, mesh=mesh, in_specs=in_specs, out_specs=out_specs, check_vma=False
    )
```

```python
import functools

import jax
import jax.numpy as jnp
from jax import lax
from jax.experimental import pallas as pl
from jax.experimental.pallas import tpu as pltpu
from jax.sharding import PartitionSpec as P

MESH = pl.DeviceIdType.MESH
F32 = jnp.float32
BF16 = jnp.bfloat16
NX, NY, NZ = 4, 8, 12
CAP = 24
SLOTS = NZ * CAP
GATE_UNIT = 65536.0
VLIM = 56


Y_ORDER = (4, 3, -3, 2, -2, 1, -1, 0)
X_ORDER = (2, 1, -1, 0)
A_UNITS = (((0, 0), (0, 1), (0, 2)), ((1, 0), (1, 1)))
B_UNITS = (((2, 0), (2, 1), (2, 2)), ((3, 0), (3, 1), (3, 2), (1, 2)))


def chains_of(n):
    half = n // 2
    return ((1, 0, half), (-1, 1, half), (1, 1, half - 1), (-1, 0, half - 1))


def kernel(
    ids_ref, codes_ref, tok_hbm, cot_hbm, wg_hbm, wu_hbm, wd_hbm,
    out_tok, out_gate, out_up, out_down,
    tok, cot, wg, wu, wd, place, send_x, send_c, recv_x, recv_c, x_full, c_full, to_gate, to_up,
    d_both, hidden, own_part, peer_out, peer_in, back_out, back_in, tok_grad,
    parts_a, parts_b, parts_a2, parts_b2, slots_a, slots_b, slots_a2, slots_b2,
    in_sem, zx_s, zx_r, zc_s, zc_r, tx_s, tx_r, tc_s, tc_r, loc_sem, p_s, p_r, back_s, back_r,
    ra_s, ra_r, rb_s, rb_r, ra2_s, ra2_r, rb2_s, rb2_r,
):
    dp = lax.axis_index("dp")
    z = lax.axis_index("expert")
    c = lax.axis_index("tensor")
    y, x = dp // NX, dp % NX
    peer = 1 - c
    cols = tok.shape[1]

    def in_blocks(src, dst, first):
        size = dst.shape[0] // 4
        return [
            pltpu.make_async_copy(
                src.at[i * size : (i + 1) * size], dst.at[i * size : (i + 1) * size], in_sem.at[first + i]
            )
            for i in range(4)
        ]

    tok_loads, cot_loads = in_blocks(tok_hbm, tok, 0), in_blocks(cot_hbm, cot, 4)
    weight_loads = [
        pltpu.make_async_copy(src, dst, in_sem.at[8 + i]) for i, (src, dst) in enumerate(((wg_hbm, wg), (wu_hbm, wu), (wd_hbm, wd)))
    ]
    for load in tok_loads:
        load.start()

    def at_z(k):
        return (dp, k, c)

    def at_x(k):
        return (y * NX + k, z, c)

    def at_y(k):
        return (k * NX + x, z, c)

    at_peer = (dp, z, peer)

    barrier = pltpu.get_barrier_semaphore()

    def greet(i, carry):
        pl.semaphore_signal(barrier, inc=1, device_id=at_z(lax.rem(z + i, NZ)), device_id_type=MESH)
        return carry

    lax.fori_loop(1, NZ, greet, 0)
    pl.semaphore_signal(barrier, inc=1, device_id=at_peer, device_id_type=MESH)
    for step in (1, NX - 1):
        pl.semaphore_signal(barrier, inc=1, device_id=at_x(lax.rem(x + step, NX)), device_id_type=MESH)
    for step in (1, NY - 1):
        pl.semaphore_signal(barrier, inc=1, device_id=at_y(lax.rem(y + step, NY)), device_id_type=MESH)

    count = ids_ref.shape[1]
    expert_row = lax.broadcasted_iota(jnp.int32, (16, count), 0)
    match = jnp.zeros((16, count), F32)
    for k in range(ids_ref.shape[0]):
        same = ids_ref[k : k + 1, :] == expert_row
        match = match + jnp.where(same, 1.0, 0.0)
    before = jnp.where(
        lax.broadcasted_iota(jnp.int32, (count, count), 0) < lax.broadcasted_iota(jnp.int32, (count, count), 1),
        1.0, 0.0,
    ).astype(BF16)
    position = jnp.dot(match.astype(BF16), before, preferred_element_type=F32)
    position = jnp.where(match > 0.5, position, -1.0)
    slot_row = lax.broadcasted_iota(jnp.int32, (CAP, count), 0).astype(F32)
    pieces = [jnp.where(position[e : e + 1, :] == slot_row, 1.0, 0.0) for e in range(NZ)]
    place[...] = jnp.concatenate(pieces, axis=0).astype(BF16)

    def z_copy(src, dst, send, recv, target, slab):
        return pltpu.make_async_remote_copy(
            src_ref=src.at[target], dst_ref=dst.at[c, slab], send_sem=send.at[target], recv_sem=recv.at[slab],
            device_id=at_z(target), device_id_type=MESH,
        )

    def t_copy(src, dst, half, send, recv, slab):
        return pltpu.make_async_remote_copy(
            src_ref=src, dst_ref=dst.at[half, slab], send_sem=send.at[slab], recv_sem=recv.at[slab],
            device_id=at_peer, device_id_type=MESH,
        )

    def turn(i):
        step = (NZ + 1 - i) // 2
        return lax.rem(z + NZ + jnp.where(i % 2 == 1, step, -step), NZ)

    def gather(table, buffer, scale):
        for block in range(cols // 256):
            part = jnp.dot(place[...], table[:, block * 256 : block * 256 + 256], preferred_element_type=F32)
            if scale is not None:
                part = scale * part
            for e in range(NZ):
                buffer[e, :, block * 256 : block * 256 + 256] = part[e * CAP : (e + 1) * CAP, :].astype(BF16)

    def send_all(src, dst, zs, zr, ts, tr, own):
        def one(i, carry):
            z_copy(src, dst, zs, zr, turn(i), z).start()
            return carry

        lax.fori_loop(1, NZ, one, 0)
        t_copy(src.at[z], dst, c, ts, tr, z).start()
        own_copy = pltpu.make_async_copy(src.at[z], dst.at[c, z], loc_sem.at[own])
        own_copy.start()
        return own_copy

    for load in tok_loads:
        load.wait()
    for load in cot_loads:
        load.start()
    gather(tok, send_x, None)
    pl.semaphore_wait(barrier, NZ - 1 + 5)
    own_x = send_all(send_x, recv_x, zx_s, zx_r, tx_s, tx_r, 0)
    gates = jnp.zeros((16, count), F32)
    for k in range(ids_ref.shape[0]):
        same = ids_ref[k : k + 1, :] == expert_row
        gates = gates + jnp.where(same, codes_ref[k : k + 1, :].astype(F32) / GATE_UNIT, 0.0)
    slot_gate = jnp.concatenate(
        [
            jnp.sum(place[e * CAP : (e + 1) * CAP, :].astype(F32) * gates[e : e + 1, :], axis=1, keepdims=True)
            for e in range(NZ)
        ],
        axis=0,
    )
    for load in cot_loads:
        load.wait()
    for load in weight_loads:
        load.start()
    gather(cot, send_c, slot_gate)
    own_c = send_all(send_c, recv_c, zc_s, zc_r, tc_s, tc_r, 1)

    slab_of = [z] + [turn(i) for i in range(1, NZ)]

    def pass_on(src, dst, zs, zr, ts, tr, low, high):
        def one(i, carry):
            slab = turn(i)
            z_copy(src, dst, zs, zr, slab, slab).wait_recv()
            t_copy(dst.at[c, slab], dst, c, ts, tr, slab).start()
            return carry

        lax.fori_loop(low, high, one, 0)

    def from_peer(src, dst, ts, tr, low, high):
        def one(i, carry):
            slab = jnp.where(i == 0, z, turn(i))
            t_copy(src.at[slab], dst, peer, ts, tr, slab).wait_recv()
            return carry

        lax.fori_loop(low, high, one, 0)

    def assemble(slabs, full, half, low, high):
        def one(b, carry):
            col = pl.multiple_of(b * 256, 256)
            rows = [slabs[half, slab_of[i], :, pl.ds(col, 256)].astype(F32) for i in range(low, high)]
            full[half, low * CAP : high * CAP, pl.ds(col, 256)] = jnp.concatenate(rows, axis=0).astype(BF16)
            return carry

        lax.fori_loop(0, cols // 256, one, 0)

    def product(full, weights, half, low, high):
        rows = pl.ds(pl.multiple_of(half * cols, cols), cols)
        return jnp.dot(full[half, low * CAP : high * CAP, :], weights[rows, :], preferred_element_type=F32)

    pass_on(send_x, recv_x, zx_s, zx_r, tx_s, tx_r, 1, NZ)
    own_x.wait()
    from_peer(send_x, recv_x, tx_s, tx_r, 0, NZ)
    weight_loads[0].wait()
    weight_loads[1].wait()
    assemble(recv_x, x_full, 0, 0, NZ)
    assemble(recv_x, x_full, 1, 0, NZ)
    gate = product(x_full, wg, 0, 0, NZ) + product(x_full, wg, 1, 0, NZ)
    up = product(x_full, wu, 0, 0, NZ) + product(x_full, wu, 1, 0, NZ)
    width = hidden.shape[1]
    sigma = jax.nn.sigmoid(gate)
    activated = gate * sigma
    hidden[...] = (activated * up).astype(BF16)
    to_gate[...] = up * sigma * (1.0 + gate * (1.0 - sigma))
    to_up[...] = activated
    weight_loads[2].wait()

    own_c.wait()
    for low, high in ((0, NZ // 2), (NZ // 2, NZ)):
        pass_on(send_c, recv_c, zc_s, zc_r, tc_s, tc_r, max(low, 1), high)
        assemble(recv_c, c_full, c, low, high)
        d_own = product(c_full, wd, c, low, high)
        from_peer(send_c, recv_c, tc_s, tc_r, low, high)
        assemble(recv_c, c_full, peer, low, high)
        d_hidden = d_own + product(c_full, wd, peer, low, high)
        held = slice(low * CAP, high * CAP)
        d_both[held, :width] = (d_hidden * to_gate[held, :]).astype(BF16)
        d_both[held, width:] = (d_hidden * to_up[held, :]).astype(BF16)

    over_rows = (((0,), (0,)), ((), ()))

    def x_place(k):
        gap = lax.rem(k - x + NX, NX)
        return jnp.where(gap == 0, 3, jnp.where(gap == 1, 1, jnp.where(gap == 2, 0, 2)))

    x_places = [x_place(k) for k in range(NX)]

    def weight_block(j, carry):
        offset = jnp.where(j % 2 == 0, -((NY - j) // 2), (NY - 1 - j) // 2)
        b = lax.rem(y + offset + NY, NY)
        side = b // (NY // 2)
        col = pl.multiple_of(lax.rem(b, NY // 2) * 256, 256)
        both = lax.dot_general(
            x_full[side, :, pl.ds(col, 256)], d_both[...], over_rows, preferred_element_type=F32
        )
        down = lax.dot_general(
            c_full[side, :, pl.ds(col, 256)], hidden[...], over_rows, preferred_element_type=F32
        )
        values = [v.astype(BF16) for v in (both[:, :width], both[:, width:], down)]
        for k in range(NX):
            for p in range(2):
                for u, (q, m) in enumerate(A_UNITS[p]):
                    row = k * 64 + q * 16
                    parts_a[p][b, x_places[k], u * 16 : u * 16 + 16, :] = values[m][row : row + 16, :]
                for u, (q, m) in enumerate(B_UNITS[p]):
                    row = k * 64 + q * 16
                    parts_b[p][k, j, u * 16 : u * 16 + 16, :] = values[m][row : row + 16, :]
        return carry

    rings = {
        "a": (NY, y, at_y, parts_a, slots_a, ra_s, ra_r, 2, 2),
        "b": (NX, x, at_x, parts_b, slots_b, rb_s, rb_r, 4, 2),
        "a2": (NX, x, at_x, parts_a2, slots_a2, ra2_s, ra2_r, 1, 1),
        "b2": (NY, y, at_y, parts_b2, slots_b2, rb2_s, rb2_r, 1, 1),
    }

    def hop(ring, i, h, g):
        n, me, at, parts, slots, send, recv, groups, size = rings[ring]
        sign, part, length = chains_of(n)[i]
        target = lax.rem(me + n + sign, n)
        dest = lax.rem(me + n + sign * (length - h), n)
        piece = pl.ds(g * size, size)
        src = parts[part].at[dest, piece] if h == 0 else slots[i].at[h - 1, piece]
        sem = (sum(l for _, _, l in chains_of(n)[:i]) + h) * groups + g
        return pltpu.make_async_remote_copy(
            src_ref=src, dst_ref=slots[i].at[h, piece], send_sem=send.at[sem], recv_sem=recv.at[sem],
            device_id=at(target), device_id_type=MESH,
        )

    def begin(ring, which, g):
        for i in which:
            hop(ring, i, 0, g).start()

    def serve(ring, which, h, g):
        n, me, at, parts, slots, send, recv, groups, size = rings[ring]
        for i in which:
            sign, part, length = chains_of(n)[i]
            hop(ring, i, h, g).wait_recv()
            if h < length - 1:
                dest = lax.rem(me + n + sign * (length - h - 1), n)
                for k in range(g * size, g * size + size):
                    total = slots[i][h, k].astype(F32) + parts[part][dest, k].astype(F32)
                    slots[i][h, k] = total.astype(BF16)
                hop(ring, i, h + 1, g).start()

    def finish(ring, g, store):
        n, me, at, parts, slots, send, recv, groups, size = rings[ring]
        for part in range(2):
            ends = [(i, l - 1) for i, (_, p, l) in enumerate(chains_of(n)) if p == part]
            for k in range(g * size, g * size + size):
                total = parts[part][me, k].astype(F32)
                for i, h in ends:
                    total = total + slots[i][h, k].astype(F32)
                store(part, k, total)

    def to_a2(part, k, total):
        parts_a2[part][lax.rem(x + NX + X_ORDER[k], NX), 0] = total.astype(BF16)

    def to_b2(part, k, total):
        parts_b2[part][lax.rem(y + NY + Y_ORDER[k], NY), 0] = total.astype(BF16)

    def to_out(units):
        def store(part, k, total):
            for u, (q, m) in enumerate(units[part]):
                out = (out_gate, out_up, out_down)[m]
                out[q * 16 : q * 16 + 16, :] = total[u * 16 : u * 16 + 16, :]

        return store

    every, long, short = (0, 1, 2, 3), (0, 1), (2, 3)

    over_width = (((1,), (1,)), ((), ()))

    def route_block(row):
        rows = pl.ds(pl.multiple_of(row, 256), 256)
        return lax.dot_general(
            d_both[:, :width], wg[rows, :], over_width, preferred_element_type=F32
        ) + lax.dot_general(d_both[:, width:], wu[rows, :], over_width, preferred_element_type=F32)

    def peer_copy(b):
        return pltpu.make_async_remote_copy(
            src_ref=peer_out.at[b], dst_ref=peer_in.at[b], send_sem=p_s.at[b], recv_sem=p_r.at[b],
            device_id=at_peer, device_id_type=MESH,
        )

    blocks = cols // 256

    def for_peer(b, carry):
        peer_out[b] = route_block(peer * cols + b * 256).astype(BF16)
        peer_copy(b).start()
        return carry

    def for_own(b, carry):
        own_part[b] = route_block(c * cols + b * 256)
        return carry

    lax.fori_loop(0, 1, weight_block, 0)
    for g in range(2):
        begin("a", long, g)
    lax.fori_loop(1, 3, weight_block, 0)
    for g in range(2):
        begin("a", short, g)
    begin("b", every, 0)
    lax.fori_loop(0, blocks, for_peer, 0)
    lax.fori_loop(3, 5, weight_block, 0)
    begin("b", every, 1)
    lax.fori_loop(0, blocks, for_own, 0)
    serve("a", long, 0, 0)
    serve("a", long, 0, 1)

    def join(b, carry):
        peer_copy(b).wait_recv()
        total = (own_part[b] + peer_in[b].astype(F32))
        col = pl.multiple_of(b * 256, 256)
        for e in range(NZ):
            back_out[slab_of[e], :, pl.ds(col, 256)] = total[e * CAP : (e + 1) * CAP, :].astype(BF16)
        return carry

    lax.fori_loop(0, blocks, join, 0)

    def back_copy(target, slab):
        return pltpu.make_async_remote_copy(
            src_ref=back_out.at[target], dst_ref=back_in.at[slab], send_sem=back_s.at[target],
            recv_sem=back_r.at[slab], device_id=at_z(target), device_id_type=MESH,
        )

    def send_back(i, carry):
        back_copy(turn(i), z).start()
        return carry

    lax.fori_loop(1, NZ, send_back, 0)
    own_back = pltpu.make_async_copy(back_out.at[z], back_in.at[z], loc_sem.at[2])
    own_back.start()
    lax.fori_loop(5, NY, weight_block, 0)

    serve("a", short, 0, 0)
    serve("b", long, 0, 0)
    begin("b", every, 2)
    serve("a", short, 0, 1)
    serve("a", long, 1, 0)
    serve("b", short, 0, 0)
    serve("b", long, 1, 0)
    finish("b", 0, to_b2)
    begin("b2", (0, 1, 2), 0)
    serve("a", long, 1, 1)
    serve("b", long, 0, 1)
    begin("b", every, 3)
    serve("a", short, 1, 0)
    serve("a", short, 1, 1)
    serve("a", long, 2, 0)
    serve("b", short, 0, 1)
    serve("b", long, 1, 1)
    finish("b", 1, to_b2)
    begin("b2", (3,), 0)
    serve("b2", (0, 1, 2), 0, 0)
    serve("a", long, 2, 1)
    serve("b", long, 0, 2)
    serve("a", short, 2, 0)
    serve("a", short, 2, 1)
    serve("b2", (0,), 1, 0)
    serve("b", short, 0, 2)
    serve("b", long, 1, 2)
    finish("b", 2, to_b2)
    serve("b2", (3,), 0, 0)
    serve("b2", (1, 2), 1, 0)
    serve("b2", (0,), 2, 0)
    serve("b", long, 0, 3)
    serve("a", long, 3, 0)
    finish("a", 0, to_a2)
    begin("a2", (0, 1, 2), 0)
    serve("a", long, 3, 1)
    finish("a", 1, to_a2)
    begin("a2", (3,), 0)
    serve("b", short, 0, 3)
    serve("b", long, 1, 3)
    finish("b", 3, to_b2)
    serve("b2", (1,), 2, 0)
    serve("b2", (3,), 1, 0)
    serve("a2", long, 0, 0)

    def arrived(i, carry):
        back_copy(turn(i), turn(i)).wait_recv()
        return carry

    lax.fori_loop(1, NZ, arrived, 0)
    own_back.wait()

    def token_block(b, carry):
        col = pl.multiple_of(b * 256, 256)
        rows = [back_in[e, :, pl.ds(col, 256)].astype(F32) for e in range(NZ)]
        rows = jnp.concatenate(rows, axis=0).astype(BF16)
        tok_grad[:, pl.ds(col, 256)] = lax.dot_general(
            place[...], rows, over_rows, preferred_element_type=F32
        ).astype(BF16)
        return carry

    lax.fori_loop(0, blocks, token_block, 0)
    tok_out = pltpu.make_async_copy(tok_grad, out_tok, loc_sem.at[3])
    tok_out.start()

    serve("a2", short, 0, 0)
    serve("a2", long, 1, 0)
    finish("a2", 0, to_out(A_UNITS))
    serve("b2", (0, 1), 3, 0)
    serve("b2", (2, 3), 2, 0)
    finish("b2", 0, to_out(B_UNITS))
    tok_out.wait()

    def sent(i, carry):
        target = turn(i)
        z_copy(send_x, recv_x, zx_s, zx_r, target, z).wait_send()
        z_copy(send_c, recv_c, zc_s, zc_r, target, z).wait_send()
        back_copy(target, z).wait_send()
        return carry

    lax.fori_loop(1, NZ, sent, 0)

    def sent_peer(i, carry):
        t_copy(send_x.at[i], recv_x, c, tx_s, tx_r, i).wait_send()
        t_copy(send_c.at[i], recv_c, c, tc_s, tc_r, i).wait_send()
        return carry

    lax.fori_loop(0, NZ, sent_peer, 0)

    def sent_blocks(b, carry):
        peer_copy(b).wait_send()
        return carry

    lax.fori_loop(0, blocks, sent_blocks, 0)
    for ring in rings:
        n, groups = rings[ring][0], rings[ring][7]
        for i, chain in enumerate(chains_of(n)):
            for h in range(chain[2]):
                for g in range(groups):
                    hop(ring, i, h, g).wait_send()


def finish_kernel(a, b, c, d, out_a, out_b, out_c, out_d, held_a, held_b, held_c, held_d, in_sems, out_sems):
    moves = [(b, held_b, out_b), (c, held_c, out_c), (d, held_d, out_d)]
    size = a.shape[0] // 4
    for i in range(4):
        part = pl.ds(i * size, size)
        moves.append((a.at[part], held_a.at[part], out_a.at[part]))
    loads = [pltpu.make_async_copy(src, buf, in_sems.at[i]) for i, (src, buf, _) in enumerate(moves)]
    stores = [pltpu.make_async_copy(buf, out, out_sems.at[i]) for i, (_, buf, out) in enumerate(moves)]
    for load in loads:
        load.start()
    for load, store in zip(loads, stores):
        load.wait()
        store.start()
    for store in stores:
        store.wait()


def per_device(tokens, cotangent, route_ids, gate_codes, w_gate, w_up, w_down):
    rows, cols = tokens.shape
    depth, width = w_gate.shape[1:]
    dma = lambda n: pltpu.SemaphoreType.DMA((n,))
    vm = pltpu.VMEM
    a_hops, b_hops = NY - 1, NX - 1

    def parts_of(n, blocks, units):
        return [vm((n, blocks, 16 * len(u), width), BF16) for u in units]

    def slots_of(n, blocks, units):
        return [vm((length, blocks, 16 * len(units[part]), width), BF16) for _, part, length in chains_of(n)]

    scratch = [
        vm((rows, cols), BF16), vm((rows, cols), BF16),
        vm((depth, width), BF16), vm((depth, width), BF16), vm((depth, width), BF16),
        vm((SLOTS, rows), BF16),
        vm((NZ, CAP, cols), BF16), vm((NZ, CAP, cols), BF16),
        vm((2, NZ, CAP, cols), BF16), vm((2, NZ, CAP, cols), BF16),
        vm((2, SLOTS, cols), BF16), vm((2, SLOTS, cols), BF16),
        vm((SLOTS, width), F32), vm((SLOTS, width), F32),
        vm((SLOTS, 2 * width), BF16), vm((SLOTS, width), BF16),
        vm((cols // 256, SLOTS, 256), F32), vm((cols // 256, SLOTS, 256), BF16), vm((cols // 256, SLOTS, 256), BF16),
        vm((NZ, CAP, cols), BF16), vm((NZ, CAP, cols), BF16),
        vm((rows, cols), BF16),
        parts_of(NY, NX, A_UNITS), parts_of(NX, NY, B_UNITS), parts_of(NX, 1, A_UNITS), parts_of(NY, 1, B_UNITS),
        slots_of(NY, NX, A_UNITS), slots_of(NX, NY, B_UNITS), slots_of(NX, 1, A_UNITS), slots_of(NY, 1, B_UNITS),
        dma(11), dma(NZ), dma(NZ), dma(NZ), dma(NZ), dma(NZ), dma(NZ), dma(NZ), dma(NZ), dma(4),
        dma(4), dma(4), dma(NZ), dma(NZ),
        dma(4 * a_hops), dma(4 * a_hops), dma(8 * b_hops), dma(8 * b_hops),
        dma(2 * b_hops), dma(2 * b_hops), dma(2 * a_hops), dma(2 * a_hops),
    ]
    in_vmem = pl.BlockSpec(memory_space=pltpu.VMEM)
    anywhere = pl.BlockSpec(memory_space=pl.ANY)
    out_rows = depth // (NX * NY)
    weight_out = jax.ShapeDtypeStruct((out_rows, width), F32)
    results = (jax.ShapeDtypeStruct((rows, cols), BF16), weight_out, weight_out, weight_out)
    made = pl.pallas_call(
        kernel,
        out_shape=results,
        in_specs=[in_vmem, in_vmem] + [anywhere] * 5,
        out_specs=(anywhere, in_vmem, in_vmem, in_vmem),
        scratch_shapes=scratch,
        compiler_params=pltpu.CompilerParams(
            collective_id=0, has_side_effects=True, vmem_limit_bytes=VLIM * 1024 * 1024
        ),
        name="moe_backward",
    )(route_ids.T, gate_codes.T, tokens, cotangent, w_gate[0], w_up[0], w_down[0])
    token_grad, grad_gate, grad_up, grad_down = pl.pallas_call(
        finish_kernel,
        out_shape=results,
        in_specs=[anywhere] * 4,
        out_specs=(anywhere,) * 4,
        scratch_shapes=[vm(r.shape, r.dtype) for r in results] + [dma(7), dma(7)],
        name="moe_outputs",
    )(*made)
    return token_grad, grad_gate[None], grad_up[None], grad_down[None]


def solution(mesh):
    in_specs = (
        P(("dp", "expert"), "tensor"),
        P(("dp", "expert"), "tensor"),
        P(("dp", "expert"), None),
        P(("dp", "expert"), None),
        P("expert", None, "tensor"),
        P("expert", None, "tensor"),
        P("expert", None, "tensor"),
    )
    out_specs = (
        P(("dp", "expert"), "tensor"),
        P("expert", "dp", "tensor"),
        P("expert", "dp", "tensor"),
        P("expert", "dp", "tensor"),
    )
    return jax.shard_map(
        per_device, mesh=mesh, in_specs=in_specs, out_specs=out_specs, check_vma=False
    )
```

```python
import functools

import jax
import jax.numpy as jnp
from jax import lax
from jax.experimental import pallas as pl
from jax.experimental.pallas import tpu as pltpu
from jax.sharding import PartitionSpec as P

MESH = pl.DeviceIdType.MESH
F32 = jnp.float32
BF16 = jnp.bfloat16
NX, NY, NZ = 4, 8, 12
CAP = 24
SLOTS = NZ * CAP
GATE_UNIT = 65536.0
VLIM = 56


Y_ORDER = (4, 3, -3, 2, -2, 1, -1, 0)
X_ORDER = (2, 1, -1, 0)
A_UNITS = (((0, 0), (0, 1), (0, 2)), ((1, 0), (1, 1)))
B_UNITS = (((2, 0), (2, 1), (2, 2)), ((3, 0), (3, 1), (3, 2), (1, 2)))


def chains_of(n):
    half = n // 2
    return ((1, 0, half), (-1, 1, half), (1, 1, half - 1), (-1, 0, half - 1))


def kernel(
    ids_ref, codes_ref, tok_hbm, cot_hbm, wg_hbm, wu_hbm, wd_hbm,
    out_tok, out_gate, out_up, out_down,
    tok, cot, wg, wu, wd, place, send_x, send_c, recv_x, recv_c, x_full, c_full, to_gate, to_up,
    d_both, hidden, own_part, peer_out, peer_in, back_out, back_in, tok_grad,
    parts_a, parts_b, parts_a2, parts_b2, slots_a, slots_b, slots_a2, slots_b2,
    in_sem, zx_s, zx_r, zc_s, zc_r, tx_s, tx_r, tc_s, tc_r, loc_sem, p_s, p_r, back_s, back_r,
    ra_s, ra_r, rb_s, rb_r, ra2_s, ra2_r, rb2_s, rb2_r,
):
    dp = lax.axis_index("dp")
    z = lax.axis_index("expert")
    c = lax.axis_index("tensor")
    y, x = dp // NX, dp % NX
    peer = 1 - c
    cols = tok.shape[1]

    def in_blocks(src, dst, first):
        size = dst.shape[0] // 4
        return [
            pltpu.make_async_copy(
                src.at[i * size : (i + 1) * size], dst.at[i * size : (i + 1) * size], in_sem.at[first + i]
            )
            for i in range(4)
        ]

    tok_loads, cot_loads = in_blocks(tok_hbm, tok, 0), in_blocks(cot_hbm, cot, 4)
    weight_loads = [
        pltpu.make_async_copy(src, dst, in_sem.at[8 + i]) for i, (src, dst) in enumerate(((wg_hbm, wg), (wu_hbm, wu), (wd_hbm, wd)))
    ]
    for load in tok_loads:
        load.start()

    def at_z(k):
        return (dp, k, c)

    def at_x(k):
        return (y * NX + k, z, c)

    def at_y(k):
        return (k * NX + x, z, c)

    at_peer = (dp, z, peer)

    barrier = pltpu.get_barrier_semaphore()

    def greet(i, carry):
        pl.semaphore_signal(barrier, inc=1, device_id=at_z(lax.rem(z + i, NZ)), device_id_type=MESH)
        return carry

    lax.fori_loop(1, NZ, greet, 0)
    pl.semaphore_signal(barrier, inc=1, device_id=at_peer, device_id_type=MESH)
    for step in (1, NX - 1):
        pl.semaphore_signal(barrier, inc=1, device_id=at_x(lax.rem(x + step, NX)), device_id_type=MESH)
    for step in (1, NY - 1):
        pl.semaphore_signal(barrier, inc=1, device_id=at_y(lax.rem(y + step, NY)), device_id_type=MESH)

    count = ids_ref.shape[1]
    expert_row = lax.broadcasted_iota(jnp.int32, (16, count), 0)
    match = jnp.zeros((16, count), F32)
    for k in range(ids_ref.shape[0]):
        same = ids_ref[k : k + 1, :] == expert_row
        match = match + jnp.where(same, 1.0, 0.0)
    before = jnp.where(
        lax.broadcasted_iota(jnp.int32, (count, count), 0) < lax.broadcasted_iota(jnp.int32, (count, count), 1),
        1.0, 0.0,
    ).astype(BF16)
    position = jnp.dot(match.astype(BF16), before, preferred_element_type=F32)
    position = jnp.where(match > 0.5, position, -1.0)
    slot_row = lax.broadcasted_iota(jnp.int32, (CAP, count), 0).astype(F32)
    pieces = [jnp.where(position[e : e + 1, :] == slot_row, 1.0, 0.0) for e in range(NZ)]
    place[...] = jnp.concatenate(pieces, axis=0).astype(BF16)

    def z_copy(src, dst, send, recv, target, slab):
        return pltpu.make_async_remote_copy(
            src_ref=src.at[target], dst_ref=dst.at[c, slab], send_sem=send.at[target], recv_sem=recv.at[slab],
            device_id=at_z(target), device_id_type=MESH,
        )

    def t_copy(src, dst, half, send, recv, slab):
        return pltpu.make_async_remote_copy(
            src_ref=src, dst_ref=dst.at[half, slab], send_sem=send.at[slab], recv_sem=recv.at[slab],
            device_id=at_peer, device_id_type=MESH,
        )

    def turn(i):
        step = (NZ + 1 - i) // 2
        return lax.rem(z + NZ + jnp.where(i % 2 == 1, step, -step), NZ)

    def gather(table, buffer, scale):
        for block in range(cols // 256):
            part = jnp.dot(place[...], table[:, block * 256 : block * 256 + 256], preferred_element_type=F32)
            if scale is not None:
                part = scale * part
            for e in range(NZ):
                buffer[e, :, block * 256 : block * 256 + 256] = part[e * CAP : (e + 1) * CAP, :].astype(BF16)

    def send_all(src, dst, zs, zr, ts, tr, own):
        def one(i, carry):
            z_copy(src, dst, zs, zr, turn(i), z).start()
            return carry

        lax.fori_loop(1, NZ, one, 0)
        t_copy(src.at[z], dst, c, ts, tr, z).start()
        own_copy = pltpu.make_async_copy(src.at[z], dst.at[c, z], loc_sem.at[own])
        own_copy.start()
        return own_copy

    for load in tok_loads:
        load.wait()
    for load in cot_loads:
        load.start()
    gather(tok, send_x, None)
    pl.semaphore_wait(barrier, NZ - 1 + 5)
    own_x = send_all(send_x, recv_x, zx_s, zx_r, tx_s, tx_r, 0)
    gates = jnp.zeros((16, count), F32)
    for k in range(ids_ref.shape[0]):
        same = ids_ref[k : k + 1, :] == expert_row
        gates = gates + jnp.where(same, codes_ref[k : k + 1, :].astype(F32) / GATE_UNIT, 0.0)
    slot_gate = jnp.concatenate(
        [
            jnp.sum(place[e * CAP : (e + 1) * CAP, :].astype(F32) * gates[e : e + 1, :], axis=1, keepdims=True)
            for e in range(NZ)
        ],
        axis=0,
    )
    for load in cot_loads:
        load.wait()
    for load in weight_loads:
        load.start()
    gather(cot, send_c, slot_gate)
    own_c = send_all(send_c, recv_c, zc_s, zc_r, tc_s, tc_r, 1)

    slab_of = [z] + [turn(i) for i in range(1, NZ)]

    def pass_on(src, dst, zs, zr, ts, tr, low, high):
        def one(i, carry):
            slab = turn(i)
            z_copy(src, dst, zs, zr, slab, slab).wait_recv()
            t_copy(dst.at[c, slab], dst, c, ts, tr, slab).start()
            return carry

        lax.fori_loop(low, high, one, 0)

    def from_peer(src, dst, ts, tr, low, high):
        def one(i, carry):
            slab = jnp.where(i == 0, z, turn(i))
            t_copy(src.at[slab], dst, peer, ts, tr, slab).wait_recv()
            return carry

        lax.fori_loop(low, high, one, 0)

    def assemble(slabs, full, half, low, high):
        def one(b, carry):
            col = pl.multiple_of(b * 256, 256)
            rows = [slabs[half, slab_of[i], :, pl.ds(col, 256)].astype(F32) for i in range(low, high)]
            full[half, low * CAP : high * CAP, pl.ds(col, 256)] = jnp.concatenate(rows, axis=0).astype(BF16)
            return carry

        lax.fori_loop(0, cols // 256, one, 0)

    def product(full, weights, half, low, high):
        rows = pl.ds(pl.multiple_of(half * cols, cols), cols)
        return jnp.dot(full[half, low * CAP : high * CAP, :], weights[rows, :], preferred_element_type=F32)

    pass_on(send_x, recv_x, zx_s, zx_r, tx_s, tx_r, 1, NZ)
    own_x.wait()
    from_peer(send_x, recv_x, tx_s, tx_r, 0, NZ)
    weight_loads[0].wait()
    weight_loads[1].wait()
    assemble(recv_x, x_full, 0, 0, NZ)
    assemble(recv_x, x_full, 1, 0, NZ)
    gate = product(x_full, wg, 0, 0, NZ) + product(x_full, wg, 1, 0, NZ)
    up = product(x_full, wu, 0, 0, NZ) + product(x_full, wu, 1, 0, NZ)
    width = hidden.shape[1]
    sigma = jax.nn.sigmoid(gate)
    activated = gate * sigma
    hidden[...] = (activated * up).astype(BF16)
    to_gate[...] = up * sigma * (1.0 + gate * (1.0 - sigma))
    to_up[...] = activated
    weight_loads[2].wait()

    own_c.wait()
    for low, high in ((0, NZ // 2), (NZ // 2, NZ)):
        pass_on(send_c, recv_c, zc_s, zc_r, tc_s, tc_r, max(low, 1), high)
        assemble(recv_c, c_full, c, low, high)
        d_own = product(c_full, wd, c, low, high)
        from_peer(send_c, recv_c, tc_s, tc_r, low, high)
        assemble(recv_c, c_full, peer, low, high)
        d_hidden = d_own + product(c_full, wd, peer, low, high)
        held = slice(low * CAP, high * CAP)
        d_both[held, :width] = (d_hidden * to_gate[held, :]).astype(BF16)
        d_both[held, width:] = (d_hidden * to_up[held, :]).astype(BF16)

    over_rows = (((0,), (0,)), ((), ()))

    def x_place(k):
        gap = lax.rem(k - x + NX, NX)
        return jnp.where(gap == 0, 3, jnp.where(gap == 1, 1, jnp.where(gap == 2, 0, 2)))

    x_places = [x_place(k) for k in range(NX)]

    def weight_block(j, carry):
        offset = jnp.where(j % 2 == 0, -((NY - j) // 2), (NY - 1 - j) // 2)
        b = lax.rem(y + offset + NY, NY)
        side = b // (NY // 2)
        col = pl.multiple_of(lax.rem(b, NY // 2) * 256, 256)
        both = lax.dot_general(
            x_full[side, :, pl.ds(col, 256)], d_both[...], over_rows, preferred_element_type=F32
        )
        down = lax.dot_general(
            c_full[side, :, pl.ds(col, 256)], hidden[...], over_rows, preferred_element_type=F32
        )
        values = [v.astype(BF16) for v in (both[:, :width], both[:, width:], down)]
        for k in range(NX):
            for p in range(2):
                for u, (q, m) in enumerate(A_UNITS[p]):
                    row = k * 64 + q * 16
                    parts_a[p][b, x_places[k], u * 16 : u * 16 + 16, :] = values[m][row : row + 16, :]
                for u, (q, m) in enumerate(B_UNITS[p]):
                    row = k * 64 + q * 16
                    parts_b[p][k, j, u * 16 : u * 16 + 16, :] = values[m][row : row + 16, :]
        return carry

    rings = {
        "a": (NY, y, at_y, parts_a, slots_a, ra_s, ra_r, 2, 2),
        "b": (NX, x, at_x, parts_b, slots_b, rb_s, rb_r, 4, 2),
        "a2": (NX, x, at_x, parts_a2, slots_a2, ra2_s, ra2_r, 1, 1),
        "b2": (NY, y, at_y, parts_b2, slots_b2, rb2_s, rb2_r, 1, 1),
    }

    def hop(ring, i, h, g):
        n, me, at, parts, slots, send, recv, groups, size = rings[ring]
        sign, part, length = chains_of(n)[i]
        target = lax.rem(me + n + sign, n)
        dest = lax.rem(me + n + sign * (length - h), n)
        piece = pl.ds(g * size, size)
        src = parts[part].at[dest, piece] if h == 0 else slots[i].at[h - 1, piece]
        sem = (sum(l for _, _, l in chains_of(n)[:i]) + h) * groups + g
        return pltpu.make_async_remote_copy(
            src_ref=src, dst_ref=slots[i].at[h, piece], send_sem=send.at[sem], recv_sem=recv.at[sem],
            device_id=at(target), device_id_type=MESH,
        )

    def begin(ring, which, g):
        for i in which:
            hop(ring, i, 0, g).start()

    def serve(ring, which, h, g):
        n, me, at, parts, slots, send, recv, groups, size = rings[ring]
        for i in which:
            sign, part, length = chains_of(n)[i]
            hop(ring, i, h, g).wait_recv()
            if h < length - 1:
                dest = lax.rem(me + n + sign * (length - h - 1), n)
                for k in range(g * size, g * size + size):
                    total = slots[i][h, k].astype(F32) + parts[part][dest, k].astype(F32)
                    slots[i][h, k] = total.astype(BF16)
                hop(ring, i, h + 1, g).start()

    def finish(ring, g, store):
        n, me, at, parts, slots, send, recv, groups, size = rings[ring]
        for part in range(2):
            ends = [(i, l - 1) for i, (_, p, l) in enumerate(chains_of(n)) if p == part]
            for k in range(g * size, g * size + size):
                total = parts[part][me, k].astype(F32)
                for i, h in ends:
                    total = total + slots[i][h, k].astype(F32)
                store(part, k, total)

    def to_a2(part, k, total):
        parts_a2[part][lax.rem(x + NX + X_ORDER[k], NX), 0] = total.astype(BF16)

    def to_b2(part, k, total):
        parts_b2[part][lax.rem(y + NY + Y_ORDER[k], NY), 0] = total.astype(BF16)

    def to_out(units):
        def store(part, k, total):
            for u, (q, m) in enumerate(units[part]):
                out = (out_gate, out_up, out_down)[m]
                out[q * 16 : q * 16 + 16, :] = total[u * 16 : u * 16 + 16, :]

        return store

    every, long, short = (0, 1, 2, 3), (0, 1), (2, 3)

    over_width = (((1,), (1,)), ((), ()))

    def route_block(row):
        rows = pl.ds(pl.multiple_of(row, 256), 256)
        return lax.dot_general(
            d_both[:, :width], wg[rows, :], over_width, preferred_element_type=F32
        ) + lax.dot_general(d_both[:, width:], wu[rows, :], over_width, preferred_element_type=F32)

    def peer_copy(b):
        return pltpu.make_async_remote_copy(
            src_ref=peer_out.at[b], dst_ref=peer_in.at[b], send_sem=p_s.at[b], recv_sem=p_r.at[b],
            device_id=at_peer, device_id_type=MESH,
        )

    blocks = cols // 256

    def for_peer(b, carry):
        peer_out[b] = route_block(peer * cols + b * 256).astype(BF16)
        peer_copy(b).start()
        return carry

    def for_own(b, carry):
        own_part[b] = route_block(c * cols + b * 256)
        return carry

    lax.fori_loop(0, 1, weight_block, 0)
    for g in range(2):
        begin("a", long, g)
    lax.fori_loop(1, 2, weight_block, 0)
    begin("b", every, 0)
    for g in range(2):
        begin("a", (2,), g)
    lax.fori_loop(2, 3, weight_block, 0)
    for g in range(2):
        begin("a", (3,), g)
    lax.fori_loop(0, blocks, for_peer, 0)
    lax.fori_loop(3, 5, weight_block, 0)
    begin("b", every, 1)
    lax.fori_loop(0, blocks, for_own, 0)
    serve("a", long, 0, 0)
    serve("a", long, 0, 1)

    def join(b, carry):
        peer_copy(b).wait_recv()
        total = (own_part[b] + peer_in[b].astype(F32))
        col = pl.multiple_of(b * 256, 256)
        for e in range(NZ):
            back_out[slab_of[e], :, pl.ds(col, 256)] = total[e * CAP : (e + 1) * CAP, :].astype(BF16)
        return carry

    lax.fori_loop(0, blocks, join, 0)

    def back_copy(target, slab):
        return pltpu.make_async_remote_copy(
            src_ref=back_out.at[target], dst_ref=back_in.at[slab], send_sem=back_s.at[target],
            recv_sem=back_r.at[slab], device_id=at_z(target), device_id_type=MESH,
        )

    def send_back(i, carry):
        back_copy(turn(i), z).start()
        return carry

    lax.fori_loop(1, NZ, send_back, 0)
    own_back = pltpu.make_async_copy(back_out.at[z], back_in.at[z], loc_sem.at[2])
    own_back.start()
    lax.fori_loop(5, NY, weight_block, 0)

    serve("a", short, 0, 0)
    serve("b", long, 0, 0)
    begin("b", every, 2)
    serve("a", short, 0, 1)
    serve("a", long, 1, 0)
    serve("b", short, 0, 0)
    serve("b", long, 1, 0)
    finish("b", 0, to_b2)
    begin("b2", (0, 1, 2), 0)
    serve("a", long, 1, 1)
    serve("b", long, 0, 1)
    begin("b", every, 3)
    serve("a", short, 1, 0)
    serve("a", short, 1, 1)
    serve("a", long, 2, 0)
    serve("b", short, 0, 1)
    serve("b", long, 1, 1)
    finish("b", 1, to_b2)
    begin("b2", (3,), 0)
    serve("b2", (0, 1, 2), 0, 0)
    serve("a", long, 2, 1)
    serve("b", long, 0, 2)
    serve("a", short, 2, 0)
    serve("a", short, 2, 1)
    serve("b2", (0,), 1, 0)
    serve("b", short, 0, 2)
    serve("b", long, 1, 2)
    finish("b", 2, to_b2)
    serve("b2", (3,), 0, 0)
    serve("b2", (1, 2), 1, 0)
    serve("b2", (0,), 2, 0)
    serve("b", long, 0, 3)
    serve("a", long, 3, 0)
    finish("a", 0, to_a2)
    begin("a2", (0, 1, 2), 0)
    serve("a", long, 3, 1)
    finish("a", 1, to_a2)
    begin("a2", (3,), 0)
    serve("b", short, 0, 3)
    serve("b", long, 1, 3)
    finish("b", 3, to_b2)
    serve("b2", (1,), 2, 0)
    serve("b2", (3,), 1, 0)
    serve("a2", long, 0, 0)

    def arrived(i, carry):
        back_copy(turn(i), turn(i)).wait_recv()
        return carry

    lax.fori_loop(1, NZ, arrived, 0)
    own_back.wait()

    def token_block(b, carry):
        col = pl.multiple_of(b * 256, 256)
        rows = [back_in[e, :, pl.ds(col, 256)].astype(F32) for e in range(NZ)]
        rows = jnp.concatenate(rows, axis=0).astype(BF16)
        tok_grad[:, pl.ds(col, 256)] = lax.dot_general(
            place[...], rows, over_rows, preferred_element_type=F32
        ).astype(BF16)
        return carry

    lax.fori_loop(0, blocks, token_block, 0)
    tok_out = pltpu.make_async_copy(tok_grad, out_tok, loc_sem.at[3])
    tok_out.start()

    serve("a2", short, 0, 0)
    serve("a2", long, 1, 0)
    finish("a2", 0, to_out(A_UNITS))
    serve("b2", (0, 1), 3, 0)
    serve("b2", (2, 3), 2, 0)
    finish("b2", 0, to_out(B_UNITS))
    tok_out.wait()

    def sent(i, carry):
        target = turn(i)
        z_copy(send_x, recv_x, zx_s, zx_r, target, z).wait_send()
        z_copy(send_c, recv_c, zc_s, zc_r, target, z).wait_send()
        back_copy(target, z).wait_send()
        return carry

    lax.fori_loop(1, NZ, sent, 0)

    def sent_peer(i, carry):
        t_copy(send_x.at[i], recv_x, c, tx_s, tx_r, i).wait_send()
        t_copy(send_c.at[i], recv_c, c, tc_s, tc_r, i).wait_send()
        return carry

    lax.fori_loop(0, NZ, sent_peer, 0)

    def sent_blocks(b, carry):
        peer_copy(b).wait_send()
        return carry

    lax.fori_loop(0, blocks, sent_blocks, 0)
    for ring in rings:
        n, groups = rings[ring][0], rings[ring][7]
        for i, chain in enumerate(chains_of(n)):
            for h in range(chain[2]):
                for g in range(groups):
                    hop(ring, i, h, g).wait_send()


def finish_kernel(a, b, c, d, out_a, out_b, out_c, out_d, held_a, held_b, held_c, held_d, in_sems, out_sems):
    moves = [(b, held_b, out_b), (c, held_c, out_c), (d, held_d, out_d)]
    size = a.shape[0] // 4
    for i in range(4):
        part = pl.ds(i * size, size)
        moves.append((a.at[part], held_a.at[part], out_a.at[part]))
    loads = [pltpu.make_async_copy(src, buf, in_sems.at[i]) for i, (src, buf, _) in enumerate(moves)]
    stores = [pltpu.make_async_copy(buf, out, out_sems.at[i]) for i, (_, buf, out) in enumerate(moves)]
    for load in loads:
        load.start()
    for load, store in zip(loads, stores):
        load.wait()
        store.start()
    for store in stores:
        store.wait()


def per_device(tokens, cotangent, route_ids, gate_codes, w_gate, w_up, w_down):
    rows, cols = tokens.shape
    depth, width = w_gate.shape[1:]
    dma = lambda n: pltpu.SemaphoreType.DMA((n,))
    vm = pltpu.VMEM
    a_hops, b_hops = NY - 1, NX - 1

    def parts_of(n, blocks, units):
        return [vm((n, blocks, 16 * len(u), width), BF16) for u in units]

    def slots_of(n, blocks, units):
        return [vm((length, blocks, 16 * len(units[part]), width), BF16) for _, part, length in chains_of(n)]

    scratch = [
        vm((rows, cols), BF16), vm((rows, cols), BF16),
        vm((depth, width), BF16), vm((depth, width), BF16), vm((depth, width), BF16),
        vm((SLOTS, rows), BF16),
        vm((NZ, CAP, cols), BF16), vm((NZ, CAP, cols), BF16),
        vm((2, NZ, CAP, cols), BF16), vm((2, NZ, CAP, cols), BF16),
        vm((2, SLOTS, cols), BF16), vm((2, SLOTS, cols), BF16),
        vm((SLOTS, width), F32), vm((SLOTS, width), F32),
        vm((SLOTS, 2 * width), BF16), vm((SLOTS, width), BF16),
        vm((cols // 256, SLOTS, 256), F32), vm((cols // 256, SLOTS, 256), BF16), vm((cols // 256, SLOTS, 256), BF16),
        vm((NZ, CAP, cols), BF16), vm((NZ, CAP, cols), BF16),
        vm((rows, cols), BF16),
        parts_of(NY, NX, A_UNITS), parts_of(NX, NY, B_UNITS), parts_of(NX, 1, A_UNITS), parts_of(NY, 1, B_UNITS),
        slots_of(NY, NX, A_UNITS), slots_of(NX, NY, B_UNITS), slots_of(NX, 1, A_UNITS), slots_of(NY, 1, B_UNITS),
        dma(11), dma(NZ), dma(NZ), dma(NZ), dma(NZ), dma(NZ), dma(NZ), dma(NZ), dma(NZ), dma(4),
        dma(4), dma(4), dma(NZ), dma(NZ),
        dma(4 * a_hops), dma(4 * a_hops), dma(8 * b_hops), dma(8 * b_hops),
        dma(2 * b_hops), dma(2 * b_hops), dma(2 * a_hops), dma(2 * a_hops),
    ]
    in_vmem = pl.BlockSpec(memory_space=pltpu.VMEM)
    anywhere = pl.BlockSpec(memory_space=pl.ANY)
    out_rows = depth // (NX * NY)
    weight_out = jax.ShapeDtypeStruct((out_rows, width), F32)
    results = (jax.ShapeDtypeStruct((rows, cols), BF16), weight_out, weight_out, weight_out)
    made = pl.pallas_call(
        kernel,
        out_shape=results,
        in_specs=[in_vmem, in_vmem] + [anywhere] * 5,
        out_specs=(anywhere, in_vmem, in_vmem, in_vmem),
        scratch_shapes=scratch,
        compiler_params=pltpu.CompilerParams(
            collective_id=0, has_side_effects=True, vmem_limit_bytes=VLIM * 1024 * 1024
        ),
        name="moe_backward",
    )(route_ids.T, gate_codes.T, tokens, cotangent, w_gate[0], w_up[0], w_down[0])
    token_grad, grad_gate, grad_up, grad_down = pl.pallas_call(
        finish_kernel,
        out_shape=results,
        in_specs=[anywhere] * 4,
        out_specs=(anywhere,) * 4,
        scratch_shapes=[vm(r.shape, r.dtype) for r in results] + [dma(7), dma(7)],
        name="moe_outputs",
    )(*made)
    return token_grad, grad_gate[None], grad_up[None], grad_down[None]


def solution(mesh):
    in_specs = (
        P(("dp", "expert"), "tensor"),
        P(("dp", "expert"), "tensor"),
        P(("dp", "expert"), None),
        P(("dp", "expert"), None),
        P("expert", None, "tensor"),
        P("expert", None, "tensor"),
        P("expert", None, "tensor"),
    )
    out_specs = (
        P(("dp", "expert"), "tensor"),
        P("expert", "dp", "tensor"),
        P("expert", "dp", "tensor"),
        P("expert", "dp", "tensor"),
    )
    return jax.shard_map(
        per_device, mesh=mesh, in_specs=in_specs, out_specs=out_specs, check_vma=False
    )
```
